256 devices in a mesh: leaf: 32 (over y, z), sub: 8 (over x, core).
Axes of the slice: x: 4, y: 4, z: 8, core: 2. Of those that a mesh axis runs over, the one named last changes fastest.
Arguments:
- rhs: float32 [8, 32, 1024, 128], P('sub', 'leaf'), may hold values from -6 to 6
- leaf_block: bfloat16 [8, 32, 1024, 1024], P('sub', 'leaf')
- leaf_inverse: bfloat16 [8, 32, 1024, 1024], P('sub', 'leaf')
- level_basis: float32 [8, 32, 5, 1024, 128], P('sub', 'leaf'), may hold values from -0.1875 to 0.1875
- level_core: float32 [8, 32, 5, 128, 128], P('sub', 'leaf')
- skeleton_basis: float32 [8, 32, 1024, 128], P('sub', 'leaf'), may hold values from -0.1875 to 0.1875
- coupling: float32 [8, 8, 128, 128], P('sub'), may hold values from -0.09375 to 0.09375
Outputs:
- solution: float32 [8, 32, 1024, 128], P('sub', 'leaf')
The draws below stay inside these ranges and needn't reach their ends.
All inputs are finite; a program needn't handle non-finite values.
Results may differ from the reference program's by a relative error of at most 0.0003.
Values sent between devices are 32-bit elements; how exact they have to be, the bound alone decides.
A program may use at most 64 MiB of HBM per device.

```python
import jax
import jax.numpy as jnp
from jax import lax

M = 1024
K = 128
R = 128
ROUNDS = 2
LEAVES = 32
NSUB = 8
LEVELS = 5


def dominant(key, center_lo, center_hi, spread):
    first, second = jax.random.split(key)
    shape = (NSUB, LEAVES, M, M)
    off = jax.random.normal(first, shape, jnp.float32) * (spread / M ** 0.5)
    diag = jax.random.uniform(second, (NSUB, LEAVES, M), jnp.float32, center_lo, center_hi)
    eye = jnp.eye(M, dtype=jnp.float32)
    return (off * (1.0 - eye) + diag[..., None] * eye).astype(jnp.bfloat16)


def draw_leaf_block(key, part):
    return dominant(jax.random.fold_in(key, 11), 1.5, 3.0, 0.5)


def draw_leaf_inverse(key, part):
    return dominant(jax.random.fold_in(key, 23), 0.3, 0.6, 0.15)


def draw_level_core(key, part):
    shape = (NSUB, LEAVES, LEVELS, K, K)
    scale = 0.3 / jnp.sqrt(K * 2.0 ** (jnp.arange(LEVELS, dtype=jnp.float32) + 1.0))
    base = jax.random.normal(key, shape, jnp.float32)
    return base * scale[None, None, :, None, None]


def shard_levels(rng, shape, cuts, least, high):
    level = 1.0
    for dim, parts in cuts:
        heights = jax.random.uniform(jax.random.fold_in(jax.random.fold_in(rng, 6), dim), (parts,), jnp.float32, least / len(cuts), high / len(cuts))
        level = level * jnp.repeat(jnp.exp(heights), shape[dim] // parts).reshape((-1,) + (1,) * (len(shape) - 1 - dim))
    return level


def scatter_about(stream_key, extent, deviation, bound, pieces=(), kind=jnp.bfloat16):
    loudness = shard_levels(stream_key, extent, pieces, -0.22, 0.18) if pieces else 1.0
    values = jax.random.normal(stream_key, extent, jnp.float32) * deviation * loudness
    return jnp.minimum(jnp.maximum(values, -bound), bound).astype(kind)


def setup_inputs(seed: int = 0) -> dict:
    streams_of = jax.random.split(jax.random.key(seed), 8)
    return {
        "rhs": scatter_about(streams_of[0], (NSUB, LEAVES, M, R), 1.0, 6.0, ((0, 8), (1, 32)), jnp.float32),
        "leaf_block": draw_leaf_block(jax.random.fold_in(streams_of[7], 71), 0),
        "leaf_inverse": draw_leaf_inverse(jax.random.fold_in(streams_of[7], 71), 0),
        "level_basis": scatter_about(streams_of[3], (NSUB, LEAVES, LEVELS, M, K), M ** -0.5, 0.1875, ((0, 8), (1, 32)), jnp.float32),
        "level_core": draw_level_core(jax.random.fold_in(streams_of[7], 71), 0),
        "skeleton_basis": scatter_about(streams_of[5], (NSUB, LEAVES, M, K), M ** -0.5, 0.1875, ((0, 8), (1, 32)), jnp.float32),
        "coupling": scatter_about(streams_of[6], (NSUB, NSUB, K, K), (4 * K * NSUB) ** -0.5, 0.09375, ((0, 8),), jnp.float32),
    }


HI = lax.Precision.HIGHEST


def inner_solve(field, leaf_inverse, level_basis, level_core):
    x = jnp.einsum('slmn,slnr->slmr', leaf_inverse.astype(jnp.float32), field, precision=HI)
    for level in range(LEVELS):
        size = 2 ** (level + 1)
        proj = jnp.einsum('slmk,slmr->slkr', level_basis[:, :, level], x, precision=HI)
        group = proj.reshape(NSUB, LEAVES // size, size, K, R).sum(axis=2)
        group = jnp.repeat(group, size, axis=1)
        moved = jnp.einsum('slkj,sljr->slkr', level_core[:, :, level], group, precision=HI)
        x = x - jnp.einsum('slmk,slkr->slmr', level_basis[:, :, level], moved, precision=HI)
    return x


def apply_operator(x, leaf_block, skeleton_basis, coupling):
    local = jnp.einsum('slmn,slnr->slmr', leaf_block.astype(jnp.float32), x, precision=HI)
    skel = jnp.einsum('slmk,slmr->skr', skeleton_basis, x, precision=HI)
    mixed = jnp.einsum('stkj,tjr->skr', coupling, skel, precision=HI)
    return local + jnp.einsum('slmk,skr->slmr', skeleton_basis, mixed, precision=HI)


def reference(rhs, leaf_block, leaf_inverse, level_basis, level_core, skeleton_basis, coupling):
    solution = inner_solve(rhs, leaf_inverse, level_basis, level_core)
    for outer in range(ROUNDS):
        remain = rhs - apply_operator(solution, leaf_block, skeleton_basis, coupling)
        solution = solution + inner_solve(remain, leaf_inverse, level_basis, level_core)
    return solution
```

```python
import jax
import jax.numpy as jnp
from jax import lax
from jax.experimental import pallas as pl
from jax.experimental.pallas import tpu as pltpu
from jax.sharding import PartitionSpec as P

ROUNDS = 2
F32, BF16 = jnp.float32, jnp.bfloat16
M, K, R = 1024, 128, 128
NL = 5
NB = NL + 1
NZ, NY, NSUB = 8, 4, 8
BLK = R // NZ
MESH = pl.DeviceIdType.MESH
NN = (((1,), (0,)), ((), ()))
NT = (((1,), (1,)), ((), ()))
TN = (((0,), (0,)), ((), ()))


def split(x):
    hi = x.astype(BF16)
    return hi, (x - hi.astype(F32)).astype(BF16)


def dot(a, b, dims=NN):
    return lax.dot_general(a, b, dims, preferred_element_type=F32)


def dot3(a, b, dims=NN):
    (ah, al), (bh, bl) = a, b
    return dot(ah, bh, dims) + (dot(ah, bl, dims) + dot(al, bh, dims))


def cols(first, last=None):
    return slice(first * K, (first + 1 if last is None else last) * K)


SETUP_PAIRS = [(3, 2), (4, 2), (5, 2), (4, 3), (5, 3), (5, 4)]


def buffers():
    out = {
        "inv": pltpu.VMEM((M, M), BF16),
        "blk": pltpu.VMEM((M, M), BF16),
        "rhs": pltpu.VMEM((M, R), F32),
        "bas": pltpu.VMEM((NB, M, K), F32),
        "core": pltpu.VMEM((NL, K, K), F32),
        "coup": pltpu.VMEM((NSUB, K, K), F32),
        "bhi": pltpu.VMEM((M, NB * K), BF16),
        "blo": pltpu.VMEM((M, NB * K), BF16),
        "gram": pltpu.VMEM((NL, K, NB * K), F32),
        "chi": pltpu.VMEM((K, NSUB * K), BF16),
        "clo": pltpu.VMEM((K, NSUB * K), BF16),
        "xcat": pltpu.VMEM((M, 2 * R), BF16),
        "x": pltpu.VMEM((M, R), F32),
        "h10": pltpu.VMEM((2, K, K), F32),
        "loads": pltpu.SemaphoreType.DMA((8,)),
    }

    def ring(tag, n2, n3, n4):
        nm = n2 + n3 + n4
        out[tag + "rs_out"] = pltpu.VMEM((NZ, nm, BLK, K), F32)
        out[tag + "rs_in"] = pltpu.VMEM((NZ - 1, nm, BLK, K), F32)
        out[tag + "y_out"] = pltpu.VMEM((n3 + n4, BLK, K), F32)
        out[tag + "y_in"] = pltpu.VMEM((NY - 1, n3 + n4, BLK, K), F32)
        out[tag + "ag_near"] = pltpu.VMEM((NZ, n2, BLK, K), F32)
        out[tag + "ag_far"] = pltpu.VMEM((NZ, n3 + n4, BLK, K), F32)

    ring("setup_", 3, 2, 1)
    for k in range(ROUNDS + 1):
        ring(f"s{k}_", 1, 1, 2 if k < ROUNDS else 1)
        out[f"s{k}_quad_out"] = pltpu.VMEM((2, R, K), F32)
        out[f"s{k}_quad_in"] = pltpu.VMEM((3, R, K), F32)
        out[f"s{k}_pair_in"] = pltpu.VMEM((R, K), F32)
        if k < ROUNDS:
            out[f"s{k}_yall"] = pltpu.VMEM((NSUB, BLK, K), F32)
            out[f"s{k}_zall"] = pltpu.VMEM((NZ, BLK, K), F32)
    return out


NSEM = 160
SCRATCH = buffers()


def kernel(rhs_h, blk_h, inv_h, bas_h, core_h, skel_h, coup_h, out_ref, *scratch):
    names = list(SCRATCH)
    b = dict(zip(names, scratch[: len(names)]))
    send_sems, recv_sems = scratch[len(names) :]

    loads = [
        (bas_h, b["bas"].at[pl.ds(0, NL)]),
        (skel_h, b["bas"].at[NL]),
        (core_h, b["core"]),
        (rhs_h, b["rhs"]),
        (inv_h, b["inv"]),
        (coup_h, b["coup"]),
        (blk_h, b["blk"]),
    ]
    loads = [pltpu.make_async_copy(s, d, b["loads"].at[i]) for i, (s, d) in enumerate(loads)]
    for copy in loads:
        copy.start()
    l_bas, l_skel, l_core, l_rhs, l_inv, l_coup, l_blk = loads

    leaf, sub = lax.axis_index("leaf"), lax.axis_index("sub")
    y, z = lax.div(leaf, NZ), lax.rem(leaf, NZ)
    row = y * NZ
    quad = row + lax.div(z, 4) * 4
    z_peers = [row + lax.rem(z + NZ - d, NZ) for d in range(1, NZ)]
    quad_peers = [quad + lax.rem(z + 4 - d, 4) for d in range(1, 4)]
    pair_peer = leaf + 1 - 2 * lax.rem(z, 2)
    y_peers = [(y + 1 - 2 * lax.rem(y, 2)) * NZ + z, lax.rem(y + 2, NY) * NZ + z, (NY - 1 - y) * NZ + z]
    sub_peers = [lax.rem(sub + NSUB - d, NSUB) for d in range(1, NSUB)]

    barrier = pltpu.get_barrier_semaphore()
    for peer in z_peers + y_peers:
        pl.semaphore_signal(barrier, inc=1, device_id={"leaf": peer}, device_id_type=MESH)
    for peer in sub_peers:
        pl.semaphore_signal(barrier, inc=1, device_id={"sub": peer}, device_id_type=MESH)

    sent = []

    def send(src, dst, where):
        i = len(sent)
        copy = pltpu.make_async_remote_copy(
            src_ref=src,
            dst_ref=dst,
            send_sem=send_sems.at[i],
            recv_sem=recv_sems.at[i],
            device_id=where,
            device_id_type=MESH,
        )
        copy.start()
        sent.append(copy)
        return copy

    far_first = [3, 2, 4, 1, 5, 0, 6]

    def ring_start(tag, mats):
        out = b[tag + "rs_out"]
        for m, mat in enumerate(mats):
            out[:, m] = mat.reshape(NZ, BLK, K)
        return [
            send(out.at[lax.rem(z + NZ - d - 1, NZ)], b[tag + "rs_in"].at[d], {"leaf": z_peers[d]})
            for d in far_first
        ]

    def ring_reduce(tag, n2, n3, copies):
        for copy in copies:
            copy.wait_recv()
        total = b[tag + "rs_out"][z]
        for d in range(NZ - 1):
            total = total + b[tag + "rs_in"][d]
        b[tag + "y_out"][...] = total[n2:]
        y_copies = [
            send(b[tag + "y_out"].at[pl.ds(f, total.shape[0] - n2 - f)],
                 b[tag + "y_in"].at[e, pl.ds(f, total.shape[0] - n2 - f)], {"leaf": y_peers[e]})
            for e, f in ((1, n3), (2, n3), (0, 0))
        ]
        near = b[tag + "ag_near"]
        near[z] = total[:n2]
        near_copies = [send(near.at[z], near.at[z], {"leaf": z_peers[d]}) for d in far_first]
        return total[n2:], y_copies, near_copies

    def ring_far(tag, n3, total, y_copies):
        for copy in y_copies:
            copy.wait_recv()
        y_in = b[tag + "y_in"]
        third = total[:n3] + y_in[0, :n3]
        fourth = (total[n3:] + y_in[0, n3:]) + (y_in[1, n3:] + y_in[2, n3:])
        return third, fourth

    def gather(ref, block, axis_peers):
        ref[z] = block
        return [send(ref.at[z], ref.at[z], {"leaf": z_peers[d]}) for d in far_first]

    def wait(copies):
        for copy in copies:
            copy.wait_recv()

    bhi, blo, gram = b["bhi"], b["blo"], b["gram"]

    l_bas.wait()
    l_skel.wait()
    for l in range(NB):
        bhi[:, cols(l)], blo[:, cols(l)] = split(b["bas"][l])
    for j in range(NL):
        right = slice((j + 1) * K, NB * K)
        here_hi, here_lo = bhi[:, cols(j)], blo[:, cols(j)]
        gram[j, :, right] = dot(here_hi, bhi[:, right], TN) + (
            dot(here_hi, blo[:, right], TN) + dot(here_lo, bhi[:, right], TN)
        )
    l_core.wait()
    core = [split(b["core"][l]) for l in range(NL)]

    def coupled(l, j):
        return dot3(core[j], split(gram[j, :, cols(l)]), TN)

    pl.semaphore_wait(barrier, len(z_peers) + len(y_peers) + len(sub_peers))
    b["h10"][0] = coupled(1, 0)
    h10_copy = send(b["h10"].at[0], b["h10"].at[1], {"leaf": pair_peer})
    setup_rs = ring_start("setup_", [coupled(l, j) for l, j in SETUP_PAIRS])

    l_coup.wait()
    for t in range(NSUB):
        b["chi"][:, cols(t)], b["clo"][:, cols(t)] = split(b["coup"][t])

    def spread(value):
        b["xcat"][:, :R], b["xcat"][:, R:] = split(value)

    def leaf_product(mat, finish):
        @pl.loop(0, M // 256)
        def _(t):
            rows = pl.ds(pl.multiple_of(t * 256, 256), 256)
            both = dot(mat[rows, :], b["xcat"][...])
            finish(rows, both[:, :R] + both[:, R:])

    def put_x(rows, value):
        b["x"][rows, :] = value

    def project():
        hi, lo = split(b["x"][...].T)
        both = dot(jnp.concatenate([hi, lo], axis=0), bhi[...])
        return both[:R] + both[R:] + dot(hi, blo[...])

    def expand(first, last, moved):
        hi, lo = split(moved)
        bh, bl = bhi[:, cols(first, last)], blo[:, cols(first, last)]
        both = dot(bh, jnp.concatenate([hi, lo], axis=0), NT)
        return both[:, :R] + both[:, R:] + dot(bl, hi, NT)

    h = {}
    l_rhs.wait()
    l_inv.wait()
    res = b["rhs"]
    for k in range(ROUNDS + 1):
        tag = f"s{k}_"
        last = k == ROUNDS
        spread(res[...])
        leaf_product(b["inv"], put_x)
        q = project()
        if k == 0:
            wait([h10_copy])
            h[1, 0] = split(b["h10"][0] + b["h10"][1])

        u0 = q[:, cols(0)]
        u1 = q[:, cols(1)] - dot3(split(u0), h[1, 0])
        out = b[tag + "quad_out"]
        out[1] = u1
        out[0] = u0
        near = [send(out.at[1], b[tag + "quad_in"].at[d], {"leaf": quad_peers[d]}) for d in (1, 2, 0)]
        near.append(send(out.at[0], b[tag + "pair_in"], {"leaf": pair_peer}))

        if k == 0:
            total, y_copies, near_copies = ring_reduce("setup_", 3, 2, setup_rs)
            third, fourth = ring_far("setup_", 2, total, y_copies)
            far_copies = gather(b["setup_ag_far"], jnp.concatenate([third, fourth], axis=0), None)

        wait(near)
        quad_in = b[tag + "quad_in"]
        g0 = u0 + b[tag + "pair_in"][...]
        g1 = (u1 + quad_in[0]) + (quad_in[1] + quad_in[2])
        m01 = jnp.concatenate([dot3(split(g0), core[0], NT), dot3(split(g1), core[1], NT)], axis=1)
        nb = NL if last else NB
        right = slice(2 * K, nb * K)
        both = jnp.concatenate([gram[0, :, right], gram[1, :, right]], axis=0)
        p = q[:, right] - dot3(split(m01), split(both))

        if k == 0:
            wait(near_copies)
            for i in range(3):
                h[SETUP_PAIRS[i]] = split(b["setup_ag_near"][:, i].reshape(K, K))
            wait(far_copies)
            for i in range(3):
                h[SETUP_PAIRS[3 + i]] = split(b["setup_ag_far"][:, i].reshape(K, K))

        u = []
        for l in range(2, nb):
            ul = p[:, cols(l - 2)]
            for j in range(2, l):
                ul = ul - dot3(u[j - 2][1], h[l, j])
            u.append((ul, split(ul)))
        rs = ring_start(tag, [ul for ul, _ in u])
        b["x"][...] -= expand(0, 2, m01)
        total, y_copies, near_copies = ring_reduce(tag, 1, 1, rs)
        third, fourth = ring_far(tag, 1, total, y_copies)
        if last:
            far = jnp.concatenate([third, fourth], axis=0)
        else:
            far = jnp.concatenate([third, fourth], axis=0)
            yall = b[tag + "yall"]
            yall[sub] = fourth[1]
            sub_copies = [send(yall.at[sub], yall.at[sub], {"sub": peer}) for peer in sub_peers]
            far = far[:2]
        ag_far = b[tag + "ag_far"]
        ag_far[z, :2] = far
        far_copies = [send(ag_far.at[z, pl.ds(0, 2)], ag_far.at[z, pl.ds(0, 2)], {"leaf": z_peers[d]}) for d in far_first]
        if not last:
            wait(sub_copies)
            hi, lo = split(jnp.concatenate([yall[t] for t in range(NSUB)], axis=1))
            both = dot(jnp.concatenate([hi, lo], axis=0), b["chi"][...], NT)
            zall = b[tag + "zall"]
            z_copies = gather(zall, both[:BLK] + both[BLK:] + dot(hi, b["clo"][...], NT), None)
        wait(near_copies)
        wait(far_copies)
        g2 = b[tag + "ag_near"][:, 0].reshape(R, K)
        g3 = ag_far[:, 0].reshape(R, K)
        g4 = ag_far[:, 1].reshape(R, K)
        moved = jnp.concatenate(
            [dot3(split(g), core[l], NT) for l, g in ((2, g2), (3, g3), (4, g4))], axis=1
        )
        dx = b["x"][...] - expand(2, NL, moved)
        if k == 0:
            out_ref[...] = dx
        else:
            out_ref[...] += dx
        if not last:
            if k == 0:
                l_blk.wait()
            spread(dx)

            def take(rows, value):
                res[rows, :] -= value

            leaf_product(b["blk"], take)
            wait(z_copies)
            res[...] -= expand(NL, NB, zall[...].reshape(R, K))

    for copy in sent:
        copy.wait_send()


def body(rhs, leaf_block, leaf_inverse, level_basis, level_core, skeleton_basis, coupling):
    hbm = pl.BlockSpec(memory_space=pl.ANY)
    out = pl.pallas_call(
        kernel,
        out_shape=jax.ShapeDtypeStruct((M, R), F32),
        in_specs=[hbm] * 7,
        out_specs=pl.BlockSpec(memory_space=pltpu.VMEM),
        scratch_shapes=[
            *SCRATCH.values(),
            pltpu.SemaphoreType.DMA((NSEM,)),
            pltpu.SemaphoreType.DMA((NSEM,)),
        ],
        compiler_params=pltpu.CompilerParams(
            collective_id=0, has_side_effects=True, vmem_limit_bytes=56 * 2**20
        ),
        cost_estimate=pl.CostEstimate(flops=8 * 10**9, bytes_accessed=10 * 10**6, transcendentals=0),
        name="ridge_rounds",
    )(
        rhs[0, 0],
        leaf_block[0, 0],
        leaf_inverse[0, 0],
        level_basis[0, 0],
        level_core[0, 0],
        skeleton_basis[0, 0],
        coupling[0],
    )
    return out[None, None]


def solution(mesh):
    return jax.shard_map(
        body,
        mesh=mesh,
        in_specs=(
            P("sub", "leaf", None, None),
            P("sub", "leaf", None, None),
            P("sub", "leaf", None, None),
            P("sub", "leaf", None, None, None),
            P("sub", "leaf", None, None, None),
            P("sub", "leaf", None, None),
            P("sub", None, None, None),
        ),
        out_specs=P("sub", "leaf", None, None),
        check_vma=False,
    )
```

```python
import jax
import jax.numpy as jnp
from jax import lax
from jax.experimental import pallas as pl
from jax.experimental.pallas import tpu as pltpu
from jax.sharding import PartitionSpec as P

ROUNDS = 2
F32, BF16 = jnp.float32, jnp.bfloat16
M, K, R = 1024, 128, 128
NL = 5
NB = NL + 1
NF = NL - 2 + 1
NZ, NY, NSUB = 8, 4, 8
BLK = R // NZ
MESH = pl.DeviceIdType.MESH
NN = (((1,), (0,)), ((), ()))
NT = (((1,), (1,)), ((), ()))
TN = (((0,), (0,)), ((), ()))


def split(x):
    hi = x.astype(BF16)
    return hi, (x - hi.astype(F32)).astype(BF16)


def dot(a, b, dims=NN):
    return lax.dot_general(a, b, dims, preferred_element_type=F32)


def dot3(a, b, dims=NN):
    (ah, al), (bh, bl) = a, b
    return dot(ah, bh, dims) + (dot(ah, bl, dims) + dot(al, bh, dims))


def cols(first, last=None):
    return slice(first * K, (first + 1 if last is None else last) * K)


def buffers():
    out = {
        "inv": pltpu.VMEM((M, M), BF16),
        "blk": pltpu.VMEM((M, M), BF16),
        "res": pltpu.VMEM((M, R), F32),
        "bas": pltpu.VMEM((NB, M, K), F32),
        "core": pltpu.VMEM((NL, K, K), F32),
        "coup": pltpu.VMEM((NSUB, K, K), F32),
        "bhi": pltpu.VMEM((M, NB * K), BF16),
        "blo": pltpu.VMEM((M, NB * K), BF16),
        "dhi": pltpu.VMEM((M, NF * K), BF16),
        "dlo": pltpu.VMEM((M, NF * K), BF16),
        "vhi": pltpu.VMEM((M, NF * K), BF16),
        "vlo": pltpu.VMEM((M, NF * K), BF16),
        "ehi": pltpu.VMEM((NF * K, NB * K), BF16),
        "elo": pltpu.VMEM((NF * K, NB * K), BF16),
        "gram": pltpu.VMEM((NL, K, NB * K), F32),
        "chi": pltpu.VMEM((K, NSUB * K), BF16),
        "clo": pltpu.VMEM((K, NSUB * K), BF16),
        "xcat": pltpu.VMEM((M, 2 * R), BF16),
        "x": pltpu.VMEM((M, R), F32),
        "x1": pltpu.VMEM((M, R), F32),
        "h10": pltpu.VMEM((2, K, K), F32),
        "loads": pltpu.SemaphoreType.DMA((NB + 5,)),
    }

    def ring(tag, near, far, reduced=True):
        out[tag + "rs_out"] = pltpu.VMEM((NZ, near + far, BLK, K), F32)
        out[tag + "rs_in"] = pltpu.VMEM((NZ - 1, near + far, BLK, K), F32)
        if far:
            out[tag + "y_out"] = pltpu.VMEM((far, BLK, K), F32)
            out[tag + "y_in"] = pltpu.VMEM((NY - 1, far, BLK, K), F32)
        if near:
            out[tag + "near"] = pltpu.VMEM((NZ, near, BLK, K), F32)
        if far and reduced:
            out[tag + "far"] = pltpu.VMEM((NZ, min(far, 2), BLK, K), F32)

    ring("h1_", 2, 1)
    ring("h2_", 1, 2)
    ring("s0y_", 0, 1, False)
    for k in range(ROUNDS + 1):
        ring(f"s{k}n_", 1, 0)
        ring(f"s{k}f_", 0, 3 if k == 1 else 2)
        out[f"s{k}_quad_out"] = pltpu.VMEM((2, R, K), F32)
        out[f"s{k}_quad_in"] = pltpu.VMEM((3, R, K), F32)
        out[f"s{k}_pair_in"] = pltpu.VMEM((R, K), F32)
        if k < ROUNDS:
            out[f"s{k}_yall"] = pltpu.VMEM((NSUB, BLK, K), F32)
            out[f"s{k}_zall"] = pltpu.VMEM((NZ, 1, BLK, K), F32)
    return out


NSEM = 200
SCRATCH = buffers()


def kernel(rhs_h, blk_h, inv_h, bas_h, core_h, skel_h, coup_h, out_ref, *scratch):
    names = list(SCRATCH)
    b = dict(zip(names, scratch[: len(names)]))
    send_sems, recv_sems = scratch[len(names) :]

    loads = [(bas_h.at[l], b["bas"].at[l]) for l in range(NL)] + [
        (skel_h, b["bas"].at[NL]),
        (core_h, b["core"]),
        (rhs_h, b["res"]),
        (inv_h, b["inv"]),
        (blk_h, b["blk"]),
        (coup_h, b["coup"]),
    ]
    loads = [pltpu.make_async_copy(s, d, b["loads"].at[i]) for i, (s, d) in enumerate(loads)]
    for copy in loads[: NB + 1]:
        copy.start()
    l_core, l_rhs, l_inv, l_blk, l_coup = loads[NB:]

    leaf, sub = lax.axis_index("leaf"), lax.axis_index("sub")
    y, z = lax.div(leaf, NZ), lax.rem(leaf, NZ)
    row = y * NZ
    quad = row + lax.div(z, 4) * 4
    z_peers = [row + lax.rem(z + NZ - d, NZ) for d in range(1, NZ)]
    quad_peers = [quad + lax.rem(z + 4 - d, 4) for d in range(1, 4)]
    pair_peer = leaf + 1 - 2 * lax.rem(z, 2)
    y_peers = [(y + 1 - 2 * lax.rem(y, 2)) * NZ + z, lax.rem(y + 2, NY) * NZ + z, (NY - 1 - y) * NZ + z]
    sub_peers = [lax.rem(sub + NSUB - d, NSUB) for d in range(1, NSUB)]

    barrier = pltpu.get_barrier_semaphore()
    for peer in z_peers + y_peers:
        pl.semaphore_signal(barrier, inc=1, device_id={"leaf": peer}, device_id_type=MESH)
    for peer in sub_peers:
        pl.semaphore_signal(barrier, inc=1, device_id={"sub": peer}, device_id_type=MESH)

    sent = []

    def send(src, dst, where):
        i = len(sent)
        copy = pltpu.make_async_remote_copy(
            src_ref=src,
            dst_ref=dst,
            send_sem=send_sems.at[i],
            recv_sem=recv_sems.at[i],
            device_id=where,
            device_id_type=MESH,
        )
        copy.start()
        sent.append(copy)
        return copy

    def wait(copies):
        for copy in copies:
            copy.wait_recv()

    far_first = [3, 2, 4, 1, 5, 0, 6]

    def rs_start(tag, mats):
        out = b[tag + "rs_out"]
        for m, mat in enumerate(mats):
            out[:, m] = mat.reshape(NZ, BLK, K)
        return [
            send(out.at[lax.rem(z + NZ - d - 1, NZ)], b[tag + "rs_in"].at[d], {"leaf": z_peers[d]})
            for d in far_first
        ]

    def rs_finish(tag, copies):
        wait(copies)
        total = b[tag + "rs_out"][z]
        for d in range(NZ - 1):
            total = total + b[tag + "rs_in"][d]
        return total

    def y_start(tag, total, two):
        n = total.shape[0]
        y_out, y_in = b[tag + "y_out"], b[tag + "y_in"]
        y_out[...] = total
        return [
            send(y_out.at[pl.ds(f, n - f)], y_in.at[e, pl.ds(f, n - f)], {"leaf": y_peers[e]})
            for e, f in ((1, two), (2, two), (0, 0))
            if n > f
        ]

    def y_finish(tag, total, two, copies):
        wait(copies)
        y_in = b[tag + "y_in"]
        parts = [total[i] + y_in[0, i] for i in range(two)]
        parts += [(total[i] + y_in[0, i]) + (y_in[1, i] + y_in[2, i]) for i in range(two, total.shape[0])]
        return parts

    def ag_start(name, blocks):
        ref = b[name]
        for i, block in enumerate(blocks):
            ref[z, i] = block
        return [send(ref.at[z], ref.at[z], {"leaf": z_peers[d]}) for d in far_first]

    def ag_finish(name, copies):
        wait(copies)
        return [b[name][:, i].reshape(R, K) for i in range(b[name].shape[1])]

    bhi, blo, gram = b["bhi"], b["blo"], b["gram"]

    for l in range(NB):
        loads[l].wait()
        bhi[:, cols(l)], blo[:, cols(l)] = split(b["bas"][l])
    l_inv.start()
    l_rhs.start()
    for j in range(NL):
        right = slice((j + 1) * K, NB * K)
        here_hi, here_lo = bhi[:, cols(j)], blo[:, cols(j)]
        gram[j, :, right] = dot(here_hi, bhi[:, right], TN) + (
            dot(here_hi, blo[:, right], TN) + dot(here_lo, bhi[:, right], TN)
        )
    l_blk.start()
    l_coup.start()
    l_core.wait()
    core = [split(b["core"][l]) for l in range(NL)]

    def coupled(l, j):
        return dot3(core[j], split(gram[j, :, cols(l)]), TN)

    b["h10"][0] = coupled(1, 0)
    h1_mats = [coupled(3, 2), coupled(4, 2), coupled(4, 3)]
    pl.semaphore_wait(barrier, len(z_peers) + len(y_peers) + len(sub_peers))
    h10_copy = send(b["h10"].at[0], b["h10"].at[1], {"leaf": pair_peer})
    h1_rs = rs_start("h1_", h1_mats)

    def spread(value):
        b["xcat"][:, :R], b["xcat"][:, R:] = split(value)

    def leaf_product(mat, finish):
        @pl.loop(0, M // 256)
        def _(t):
            rows = pl.ds(pl.multiple_of(t * 256, 256), 256)
            both = dot(mat[rows, :], b["xcat"][...])
            finish(rows, both[:, :R] + both[:, R:])

    def put_x(rows, value):
        b["x"][rows, :] = value

    def reduce_res(rows, value):
        b["res"][rows, :] -= value

    def project():
        hi, lo = split(b["x"][...].T)
        both = dot(jnp.concatenate([hi, lo], axis=0), bhi[...])
        return both[:R] + both[R:] + dot(hi, blo[...])

    def expand(high, low, where, moved):
        hi, lo = split(moved)
        both = dot(high[:, where], jnp.concatenate([hi, lo], axis=0), NT)
        return both[:, :R] + both[:, R:] + dot(low[:, where], hi, NT)

    def composed(where, moved):
        hi, lo = split(moved)
        both = dot(jnp.concatenate([hi, lo], axis=0), b["ehi"][where, :])
        return both[:R] + both[R:] + dot(hi, b["elo"][where, :])

    def block_bases():
        @pl.loop(0, M // 256)
        def _(t):
            rows = pl.ds(pl.multiple_of(t * 256, 256), 256)
            some = cols(2, NL)
            value = dot(b["blk"][rows, :], bhi[:, some]) + dot(b["blk"][rows, :], blo[:, some])
            b["dhi"][rows, cols(0, NF - 1)], b["dlo"][rows, cols(0, NF - 1)] = split(value)

        b["dhi"][:, cols(NF - 1)] = bhi[:, cols(NL)]
        b["dlo"][:, cols(NF - 1)] = blo[:, cols(NL)]

    def inverse_bases(first, last):
        @pl.loop(first, last)
        def _(t):
            rows = pl.ds(pl.multiple_of(t * 256, 256), 256)
            value = dot(b["inv"][rows, :], b["dhi"][...]) + dot(b["inv"][rows, :], b["dlo"][...])
            b["vhi"][rows, :], b["vlo"][rows, :] = split(value)

    def project_bases(first, last):
        for c in range(first, last):
            hi, lo = b["vhi"][:, cols(c)], b["vlo"][:, cols(c)]
            value = dot(hi, bhi[...], TN) + (dot(hi, blo[...], TN) + dot(lo, bhi[...], TN))
            b["ehi"][cols(c), :], b["elo"][cols(c), :] = split(value)

    h = {}

    def level_start(k, q):
        u0 = q[:, cols(0)]
        u1 = q[:, cols(1)] - dot3(split(u0), h[1, 0])
        out = b[f"s{k}_quad_out"]
        out[1] = u1
        out[0] = u0
        copies = [
            send(out.at[1], b[f"s{k}_quad_in"].at[d], {"leaf": quad_peers[d]}) for d in (1, 2, 0)
        ]
        return u0, u1, copies + [send(out.at[0], b[f"s{k}_pair_in"], {"leaf": pair_peer})]

    def level_finish(k, q, nb, started):
        u0, u1, copies = started
        wait(copies)
        quad_in = b[f"s{k}_quad_in"]
        g0 = u0 + b[f"s{k}_pair_in"][...]
        g1 = (u1 + quad_in[0]) + (quad_in[1] + quad_in[2])
        m01 = jnp.concatenate([dot3(split(g0), core[0], NT), dot3(split(g1), core[1], NT)], axis=1)
        right = slice(2 * K, nb * K)
        both = jnp.concatenate([gram[0, :, right], gram[1, :, right]], axis=0)
        return m01, q[:, right] - dot3(split(m01), split(both))

    def corrected(p, l, u):
        ul = p[:, cols(l - 2)]
        for j in range(2, l):
            ul = ul - dot3(u[j], h[l, j])
        u[l] = split(ul)
        return ul

    def partial(m01):
        x1 = b["x"][...] - expand(bhi, blo, cols(0, 2), m01)
        b["x1"][...] = x1
        spread(x1)
        leaf_product(b["blk"], reduce_res)
        spread(b["res"][...])
        leaf_product(b["inv"], put_x)
        return project()

    def moved_of(near, far):
        return jnp.concatenate(
            [dot3(split(g), core[l], NT) for l, g in zip((2, 3, 4), (near[0], far[0], far[1]))], axis=1
        )

    def sub_start(k, block):
        yall = b[f"s{k}_yall"]
        yall[sub] = block
        return [send(yall.at[sub], yall.at[sub], {"sub": peer}) for peer in sub_peers]

    def sub_finish(k, copies):
        wait(copies)
        yall = b[f"s{k}_yall"]
        hi, lo = split(jnp.concatenate([yall[t] for t in range(NSUB)], axis=1))
        both = dot(jnp.concatenate([hi, lo], axis=0), b["chi"][...], NT)
        return ag_start(f"s{k}_zall", [both[:BLK] + both[BLK:] + dot(hi, b["clo"][...], NT)])

    def carry(moved, mixed):
        all_moved = jnp.concatenate([moved, -mixed], axis=1)
        b["x"][...] += expand(b["vhi"], b["vlo"], cols(0, NF), all_moved)
        b["res"][...] += expand(b["dhi"], b["dlo"], cols(0, NF), all_moved)

    l_rhs.wait()
    l_inv.wait()
    spread(b["res"][...])
    leaf_product(b["inv"], put_x)
    q = project()
    wait([h10_copy])
    h[1, 0] = split(b["h10"][0] + b["h10"][1])
    started = level_start(0, q)
    h2_rs = rs_start("h2_", [coupled(5, 2), coupled(5, 3), coupled(5, 4)])
    l_blk.wait()
    block_bases()
    l_coup.wait()
    for t in range(NSUB):
        b["chi"][:, cols(t)], b["clo"][:, cols(t)] = split(b["coup"][t])
    total = rs_finish("h1_", h1_rs)
    h1_total = total[2:]
    h1_y = y_start("h1_", h1_total, 1)
    h1_near = ag_start("h1_near", [total[0], total[1]])
    inverse_bases(0, 2)
    h1_far = ag_start("h1_far", y_finish("h1_", h1_total, 1, h1_y))
    total = rs_finish("h2_", h2_rs)
    h2_total = total[1:]
    h2_y = y_start("h2_", h2_total, 1)
    h2_near = ag_start("h2_near", [total[0]])
    inverse_bases(2, 4)
    m01, p = level_finish(0, q, NB, started)
    h2_far = ag_start("h2_far", y_finish("h2_", h2_total, 1, h2_y))
    h[3, 2], h[4, 2] = (split(a) for a in ag_finish("h1_near", h1_near))
    (h[4, 3],) = (split(a) for a in ag_finish("h1_far", h1_far))
    u = {}
    near_rs = rs_start("s0n_", [corrected(p, 2, u)])
    far_rs = rs_start("s0f_", [corrected(p, 3, u), corrected(p, 4, u)])
    q = partial(m01)
    (h[5, 2],) = (split(a) for a in ag_finish("h2_near", h2_near))
    h[5, 3], h[5, 4] = (split(a) for a in ag_finish("h2_far", h2_far))
    skel_rs = rs_start("s0y_", [corrected(p, 5, u)])
    far_total = rs_finish("s0f_", far_rs)
    far_y = y_start("s0f_", far_total, 1)
    near_ag = ag_start("s0n_near", [rs_finish("s0n_", near_rs)[0]])
    project_bases(0, 2)
    far_ag = ag_start("s0f_far", y_finish("s0f_", far_total, 1, far_y))
    skel_total = rs_finish("s0y_", skel_rs)
    skel_y = y_start("s0y_", skel_total, 0)
    project_bases(2, 4)
    sub_copies = sub_start(0, y_finish("s0y_", skel_total, 0, skel_y)[0])
    moved = moved_of(ag_finish("s0n_near", near_ag), ag_finish("s0f_far", far_ag))
    q = q + composed(cols(0, NF - 1), moved)
    mixed_copies = sub_finish(0, sub_copies)
    out_ref[...] = b["x1"][...] - expand(bhi, blo, cols(2, NL), moved)

    (mixed,) = ag_finish("s0_zall", mixed_copies)
    q = q - composed(cols(NF - 1), mixed)
    started = level_start(1, q)
    carry(moved, mixed)
    m01, p = level_finish(1, q, NB, started)
    u = {}
    near_rs = rs_start("s1n_", [corrected(p, 2, u)])
    far_rs = rs_start("s1f_", [corrected(p, l, u) for l in (3, 4, 5)])
    q = partial(m01)
    far_total = rs_finish("s1f_", far_rs)
    far_y = y_start("s1f_", far_total, 1)
    near_ag = ag_start("s1n_near", [rs_finish("s1n_", near_rs)[0]])
    far = y_finish("s1f_", far_total, 1, far_y)
    sub_copies = sub_start(1, far[2])
    far_ag = ag_start("s1f_far", far[:2])
    mixed_copies = sub_finish(1, sub_copies)
    moved = moved_of(ag_finish("s1n_near", near_ag), ag_finish("s1f_far", far_ag))
    q = q + composed(cols(0, NF - 1), moved)
    out_ref[...] += b["x1"][...] - expand(bhi, blo, cols(2, NL), moved)

    (mixed,) = ag_finish("s1_zall", mixed_copies)
    q = q - composed(cols(NF - 1), mixed)
    started = level_start(2, q)
    all_moved = jnp.concatenate([moved, -mixed], axis=1)
    b["x"][...] += expand(b["vhi"], b["vlo"], cols(0, NF), all_moved)
    m01, p = level_finish(2, q, NL, started)
    u = {}
    near_rs = rs_start("s2n_", [corrected(p, 2, u)])
    far_rs = rs_start("s2f_", [corrected(p, l, u) for l in (3, 4)])
    out_ref[...] += b["x"][...] - expand(bhi, blo, cols(0, 2), m01)
    far_total = rs_finish("s2f_", far_rs)
    far_y = y_start("s2f_", far_total, 1)
    near_ag = ag_start("s2n_near", [rs_finish("s2n_", near_rs)[0]])
    far_ag = ag_start("s2f_far", y_finish("s2f_", far_total, 1, far_y))
    moved = moved_of(ag_finish("s2n_near", near_ag), ag_finish("s2f_far", far_ag))
    out_ref[...] -= expand(bhi, blo, cols(2, NL), moved)

    for copy in sent:
        copy.wait_send()


def body(rhs, leaf_block, leaf_inverse, level_basis, level_core, skeleton_basis, coupling):
    hbm = pl.BlockSpec(memory_space=pl.ANY)
    out = pl.pallas_call(
        kernel,
        out_shape=jax.ShapeDtypeStruct((M, R), F32),
        in_specs=[hbm] * 7,
        out_specs=pl.BlockSpec(memory_space=pltpu.VMEM),
        scratch_shapes=[
            *SCRATCH.values(),
            pltpu.SemaphoreType.DMA((NSEM,)),
            pltpu.SemaphoreType.DMA((NSEM,)),
        ],
        compiler_params=pltpu.CompilerParams(
            collective_id=0, has_side_effects=True, vmem_limit_bytes=56 * 2**20
        ),
        cost_estimate=pl.CostEstimate(flops=8 * 10**9, bytes_accessed=10 * 10**6, transcendentals=0),
        name="ridge_rounds",
    )(
        rhs[0, 0],
        leaf_block[0, 0],
        leaf_inverse[0, 0],
        level_basis[0, 0],
        level_core[0, 0],
        skeleton_basis[0, 0],
        coupling[0],
    )
    return out[None, None]


def solution(mesh):
    return jax.shard_map(
        body,
        mesh=mesh,
        in_specs=(
            P("sub", "leaf", None, None),
            P("sub", "leaf", None, None),
            P("sub", "leaf", None, None),
            P("sub", "leaf", None, None, None),
            P("sub", "leaf", None, None, None),
            P("sub", "leaf", None, None),
            P("sub", None, None, None),
        ),
        out_specs=P("sub", "leaf", None, None),
        check_vma=False,
    )
```

```python
import jax
import jax.numpy as jnp
from jax import lax
from jax.experimental import pallas as pl
from jax.experimental.pallas import tpu as pltpu
from jax.sharding import PartitionSpec as P

ROUNDS = 2
F32, BF16 = jnp.float32, jnp.bfloat16
M, K, R = 1024, 128, 128
NL = 5
NB = NL + 1
NF = NL - 2 + 1
NZ, NY, NSUB = 8, 4, 8
NH = 1
RH = R // NH
MESH = pl.DeviceIdType.MESH
NN = (((1,), (0,)), ((), ()))
NT = (((1,), (1,)), ((), ()))
TN = (((0,), (0,)), ((), ()))


def split(x):
    hi = x.astype(BF16)
    return hi, (x - hi.astype(F32)).astype(BF16)


def dot(a, b, dims=NN):
    return lax.dot_general(a, b, dims, preferred_element_type=F32)


def dot3(a, b, dims=NN):
    (ah, al), (bh, bl) = a, b
    return dot(ah, bh, dims) + (dot(ah, bl, dims) + dot(al, bh, dims))


def cols(first, last=None):
    return slice(first * K, (first + 1 if last is None else last) * K)


def buffers():
    out = {
        "inv": pltpu.VMEM((M, M), BF16),
        "blk": pltpu.VMEM((M, M), BF16),
        "res": pltpu.VMEM((M, R), F32),
        "bas": pltpu.VMEM((NB, M, K), F32),
        "core": pltpu.VMEM((NL, K, K), F32),
        "coup": pltpu.VMEM((NSUB, K, K), F32),
        "bhi": pltpu.VMEM((M, NB * K), BF16),
        "blo": pltpu.VMEM((M, NB * K), BF16),
        "dhi": pltpu.VMEM((M, NF * K), BF16),
        "dlo": pltpu.VMEM((M, NF * K), BF16),
        "vhi": pltpu.VMEM((M, NF * K), BF16),
        "vlo": pltpu.VMEM((M, NF * K), BF16),
        "ehi": pltpu.VMEM((NF * K, NB * K), BF16),
        "elo": pltpu.VMEM((NF * K, NB * K), BF16),
        "gram": pltpu.VMEM((NL, K, NB * K), F32),
        "chi": pltpu.VMEM((K, NSUB * K), BF16),
        "clo": pltpu.VMEM((K, NSUB * K), BF16),
        "xcat": pltpu.VMEM((M, 2 * R), BF16),
        "x": pltpu.VMEM((M, R), F32),
        "x1": pltpu.VMEM((M, R), F32),
        "h10": pltpu.VMEM((2, K, K), F32),
        "loads": pltpu.SemaphoreType.DMA((NB + 5,)),
    }

    def ring(tag, near, far, back, blk):
        out[tag + "rs_out"] = pltpu.VMEM((NZ, near + far, blk, K), F32)
        out[tag + "rs_in"] = pltpu.VMEM((NZ - 1, near + far, blk, K), F32)
        if far:
            out[tag + "y_out"] = pltpu.VMEM((far, blk, K), F32)
            out[tag + "y_in"] = pltpu.VMEM((NY - 1, far, blk, K), F32)
        out[tag + "ag"] = pltpu.VMEM((NZ, near + back, blk, K), F32)

    ring("hf_", 0, 3, 3, K // NZ)
    ring("hn_", 3, 0, 0, K // NZ)
    for k in range(ROUNDS + 1):
        for p in range(NH):
            ring(f"s{k}n{p}_", 1, 0, 0, RH // NZ)
            ring(f"s{k}f{p}_", 0, 3 if k < ROUNDS else 2, 2, RH // NZ)
            out[f"s{k}_quad_out{p}"] = pltpu.VMEM((2, RH, K), F32)
            out[f"s{k}_quad_in{p}"] = pltpu.VMEM((3, RH, K), F32)
            out[f"s{k}_pair_in{p}"] = pltpu.VMEM((RH, K), F32)
            if k < ROUNDS:
                out[f"s{k}_yall{p}"] = pltpu.VMEM((NSUB, RH // NZ, K), F32)
                out[f"s{k}_zall{p}"] = pltpu.VMEM((NZ, 1, RH // NZ, K), F32)
    return out


NSEM = 160 + 140 * NH
SCRATCH = buffers()


def kernel(rhs_h, blk_h, inv_h, bas_h, core_h, skel_h, coup_h, out_ref, *scratch):
    names = list(SCRATCH)
    b = dict(zip(names, scratch[: len(names)]))
    send_sems, recv_sems = scratch[len(names) :]

    loads = [(bas_h.at[l], b["bas"].at[l]) for l in range(NL)] + [
        (skel_h, b["bas"].at[NL]),
        (core_h, b["core"]),
        (rhs_h, b["res"]),
        (inv_h, b["inv"]),
        (blk_h, b["blk"]),
        (coup_h, b["coup"]),
    ]
    loads = [pltpu.make_async_copy(s, d, b["loads"].at[i]) for i, (s, d) in enumerate(loads)]
    for copy in loads[: NB + 1]:
        copy.start()
    l_core, l_rhs, l_inv, l_blk, l_coup = loads[NB:]

    leaf, sub = lax.axis_index("leaf"), lax.axis_index("sub")
    y, z = lax.div(leaf, NZ), lax.rem(leaf, NZ)
    row = y * NZ
    quad = row + lax.div(z, 4) * 4
    z_peers = [row + lax.rem(z + NZ - d, NZ) for d in range(1, NZ)]
    quad_peers = [quad + lax.rem(z + 4 - d, 4) for d in range(1, 4)]
    pair_peer = leaf + 1 - 2 * lax.rem(z, 2)
    y_peers = [(y + 1 - 2 * lax.rem(y, 2)) * NZ + z, lax.rem(y + 2, NY) * NZ + z, (NY - 1 - y) * NZ + z]
    sub_peers = [lax.rem(sub + NSUB - d, NSUB) for d in range(1, NSUB)]

    barrier = pltpu.get_barrier_semaphore()
    for peer in z_peers + y_peers:
        pl.semaphore_signal(barrier, inc=1, device_id={"leaf": peer}, device_id_type=MESH)
    for peer in sub_peers:
        pl.semaphore_signal(barrier, inc=1, device_id={"sub": peer}, device_id_type=MESH)

    sent = []

    def send(src, dst, where):
        i = len(sent)
        copy = pltpu.make_async_remote_copy(
            src_ref=src,
            dst_ref=dst,
            send_sem=send_sems.at[i],
            recv_sem=recv_sems.at[i],
            device_id=where,
            device_id_type=MESH,
        )
        copy.start()
        sent.append(copy)
        return copy

    def wait(copies):
        for copy in copies:
            copy.wait_recv()

    far_first = [3, 2, 4, 1, 5, 0, 6]

    def rs_store(tag, mats):
        for m, mat in enumerate(mats):
            b[tag + "rs_out"][:, m] = mat.reshape(NZ, mat.shape[0] // NZ, K)

    def rs_start(tag, mats):
        rs_store(tag, mats)
        out = b[tag + "rs_out"]
        return [
            send(out.at[lax.rem(z + NZ - d - 1, NZ)], b[tag + "rs_in"].at[d], {"leaf": z_peers[d]})
            for d in far_first
        ]

    def rs_finish(tag, copies):
        wait(copies)
        total = b[tag + "rs_out"][z]
        for d in range(NZ - 1):
            total = total + b[tag + "rs_in"][d]
        return total

    def y_start(tag, total, two):
        n = total.shape[0]
        y_out, y_in = b[tag + "y_out"], b[tag + "y_in"]
        y_out[...] = total
        return [
            send(y_out.at[pl.ds(f, n - f)], y_in.at[e, pl.ds(f, n - f)], {"leaf": y_peers[e]})
            for e, f in ((1, two), (2, two), (0, 0))
            if n > f
        ]

    def y_finish(tag, total, two, copies):
        wait(copies)
        y_in = b[tag + "y_in"]
        parts = [total[i] + y_in[0, i] for i in range(two)]
        parts += [(total[i] + y_in[0, i]) + (y_in[1, i] + y_in[2, i]) for i in range(two, total.shape[0])]
        return parts

    def ag_start(name, blocks):
        ref = b[name]
        for i, block in enumerate(blocks):
            ref[z, i] = block
        return [send(ref.at[z], ref.at[z], {"leaf": z_peers[d]}) for d in far_first]

    def ag_finish(name, copies):
        wait(copies)
        ref = b[name]
        return [ref[:, i].reshape(NZ * ref.shape[2], K) for i in range(ref.shape[1])]

    bhi, blo, gram = b["bhi"], b["blo"], b["gram"]

    for l in range(NB):
        loads[l].wait()
        bhi[:, cols(l)], blo[:, cols(l)] = split(b["bas"][l])
    l_inv.start()
    l_rhs.start()
    for j in range(NL):
        right = slice((j + 1) * K, NB * K)
        here_hi, here_lo = bhi[:, cols(j)], blo[:, cols(j)]
        gram[j, :, right] = dot(here_hi, bhi[:, right], TN) + (
            dot(here_hi, blo[:, right], TN) + dot(here_lo, bhi[:, right], TN)
        )
    l_blk.start()
    l_coup.start()
    l_core.wait()
    core = [split(b["core"][l]) for l in range(NL)]

    def coupled(l, j):
        return dot3(core[j], split(gram[j, :, cols(l)]), TN)

    b["h10"][0] = coupled(1, 0)
    hf_mats = [coupled(4, 3), coupled(5, 3), coupled(5, 4)]
    pl.semaphore_wait(barrier, len(z_peers) + len(y_peers) + len(sub_peers))
    h10_copy = send(b["h10"].at[0], b["h10"].at[1], {"leaf": pair_peer})
    hf_rs = rs_start("hf_", hf_mats)

    def spread(value):
        b["xcat"][:, :R], b["xcat"][:, R:] = split(value)

    def leaf_product(mat, finish):
        @pl.loop(0, M // 256)
        def _(t):
            rows = pl.ds(pl.multiple_of(t * 256, 256), 256)
            both = dot(mat[rows, :], b["xcat"][...])
            finish(rows, both[:, :R] + both[:, R:])

    def put_x(rows, value):
        b["x"][rows, :] = value

    def reduce_res(rows, value):
        b["res"][rows, :] -= value

    def project():
        hi, lo = split(b["x"][...].T)
        both = dot(jnp.concatenate([hi, lo], axis=0), bhi[...])
        return both[:R] + both[R:] + dot(hi, blo[...])

    def expand(high, low, where, moved):
        hi, lo = split(moved)
        both = dot(high[:, where], jnp.concatenate([hi, lo], axis=0), NT)
        return both[:, :R] + both[:, R:] + dot(low[:, where], hi, NT)

    def composed(where, moved):
        hi, lo = split(moved)
        both = dot(jnp.concatenate([hi, lo], axis=0), b["ehi"][where, :])
        return both[: moved.shape[0]] + both[moved.shape[0] :] + dot(hi, b["elo"][where, :])

    def block_bases():
        @pl.loop(0, M // 256)
        def _(t):
            rows = pl.ds(pl.multiple_of(t * 256, 256), 256)
            some = cols(2, NL)
            value = dot(b["blk"][rows, :], bhi[:, some]) + dot(b["blk"][rows, :], blo[:, some])
            b["dhi"][rows, cols(0, NF - 1)], b["dlo"][rows, cols(0, NF - 1)] = split(value)

        b["dhi"][:, cols(NF - 1)] = bhi[:, cols(NL)]
        b["dlo"][:, cols(NF - 1)] = blo[:, cols(NL)]

    def inverse_bases(first, last):
        @pl.loop(first, last)
        def _(t):
            rows = pl.ds(pl.multiple_of(t * 256, 256), 256)
            value = dot(b["inv"][rows, :], b["dhi"][...]) + dot(b["inv"][rows, :], b["dlo"][...])
            b["vhi"][rows, :], b["vlo"][rows, :] = split(value)

    def project_bases(first, last):
        for c in range(first, last):
            hi, lo = b["vhi"][:, cols(c)], b["vlo"][:, cols(c)]
            value = dot(hi, bhi[...], TN) + (dot(hi, blo[...], TN) + dot(lo, bhi[...], TN))
            b["ehi"][cols(c), :], b["elo"][cols(c), :] = split(value)

    h = {}

    def level_start(k, p, q):
        u0 = q[:, cols(0)]
        u1 = q[:, cols(1)] - dot3(split(u0), h[1, 0])
        out = b[f"s{k}_quad_out{p}"]
        out[1] = u1
        out[0] = u0
        copies = [
            send(out.at[1], b[f"s{k}_quad_in{p}"].at[d], {"leaf": quad_peers[d]}) for d in (1, 2, 0)
        ]
        return u0, u1, copies + [send(out.at[0], b[f"s{k}_pair_in{p}"], {"leaf": pair_peer})]

    def level_finish(k, p, q, nb, started):
        u0, u1, copies = started
        wait(copies)
        quad_in = b[f"s{k}_quad_in{p}"]
        g0 = u0 + b[f"s{k}_pair_in{p}"][...]
        g1 = (u1 + quad_in[0]) + (quad_in[1] + quad_in[2])
        m01 = jnp.concatenate([dot3(split(g0), core[0], NT), dot3(split(g1), core[1], NT)], axis=1)
        right = slice(2 * K, nb * K)
        both = jnp.concatenate([gram[0, :, right], gram[1, :, right]], axis=0)
        return m01, q[:, right] - dot3(split(m01), split(both))

    def corrected(field, l, u):
        ul = field[:, cols(l - 2)]
        for j in sorted(u):
            ul = ul - dot3(u[j], h[l, j])
        u[l] = split(ul)
        return ul

    def partial(m01):
        x1 = b["x"][...] - expand(bhi, blo, cols(0, 2), m01)
        b["x1"][...] = x1
        spread(x1)
        leaf_product(b["blk"], reduce_res)
        spread(b["res"][...])
        leaf_product(b["inv"], put_x)
        return project()

    def moved_of(level, g):
        return dot3(split(g), core[level], NT)

    def sub_start(k, p, block):
        yall = b[f"s{k}_yall{p}"]
        yall[sub] = block
        return [send(yall.at[sub], yall.at[sub], {"sub": peer}) for peer in sub_peers]

    def sub_finish(k, p, copies):
        wait(copies)
        yall = b[f"s{k}_yall{p}"]
        hi, lo = split(jnp.concatenate([yall[t] for t in range(NSUB)], axis=1))
        if NH == 1:
            both = dot(jnp.concatenate([hi, lo], axis=0), b["chi"][...], NT)
            value = both[: RH // NZ] + both[RH // NZ :] + dot(hi, b["clo"][...], NT)
        else:
            value = dot(hi, b["chi"][...], NT) + (dot(lo, b["chi"][...], NT) + dot(hi, b["clo"][...], NT))
        return ag_start(f"s{k}_zall{p}", [value])

    def carry(moved, mixed, further):
        all_moved = jnp.concatenate([moved, -mixed], axis=1)
        b["x"][...] += expand(b["vhi"], b["vlo"], cols(0, NF), all_moved)
        if further:
            b["res"][...] += expand(b["dhi"], b["dlo"], cols(0, NF), all_moved)

    parts = range(NH)

    def part(value, p):
        return value[p * RH : (p + 1) * RH]

    def whole(values):
        return jnp.concatenate(list(values), axis=0)

    def far_reduce(k, rs):
        totals = [None] * NH
        ys = [None] * NH
        for p in parts:
            totals[p] = rs_finish(f"s{k}f{p}_", rs[p])
            ys[p] = y_start(f"s{k}f{p}_", totals[p], 1)
        return totals, ys

    def far_gather(k, totals, ys):
        subs, ags = [None] * NH, [None] * NH
        for p in parts:
            sums = y_finish(f"s{k}f{p}_", totals[p], 1, ys[p])
            if k < ROUNDS:
                subs[p] = sub_start(k, p, sums[2])
            ags[p] = ag_start(f"s{k}f{p}_ag", sums[:2])
        return subs, ags

    l_rhs.wait()
    l_inv.wait()
    spread(b["res"][...])
    leaf_product(b["inv"], put_x)
    q = project()
    wait([h10_copy])
    h[1, 0] = split(b["h10"][0] + b["h10"][1])
    q = [part(q, p) for p in parts]
    started = [level_start(0, p, q[p]) for p in parts]
    rs_store("hn_", [coupled(3, 2), coupled(4, 2), coupled(5, 2)])
    l_blk.wait()
    block_bases()
    l_coup.wait()
    for t in range(NSUB):
        b["chi"][:, cols(t)], b["clo"][:, cols(t)] = split(b["coup"][t])
    hf_total = rs_finish("hf_", hf_rs)
    hf_y = y_start("hf_", hf_total, 2)
    fields, m01s, near_rs = [], [], []
    for p in parts:
        m01, field = level_finish(0, p, q[p], NB, started[p])
        m01s.append(m01)
        fields.append(field)
        near_rs.append(rs_start(f"s0n{p}_", [field[:, cols(0)]]))
    hf_ag = ag_start("hf_ag", y_finish("hf_", hf_total, 2, hf_y))
    inverse_bases(0, 3)
    near_ag = [ag_start(f"s0n{p}_ag", [rs_finish(f"s0n{p}_", near_rs[p])[0]]) for p in parts]
    hn_rs = rs_start("hn_", [])
    inverse_bases(3, 4)
    hf = ag_finish("hf_ag", hf_ag)
    for i, pair in enumerate([(4, 3), (5, 3), (5, 4)]):
        h[pair] = split(hf[i])
    m2s, far_rs = [], []
    for p in parts:
        (g2,) = ag_finish(f"s0n{p}_ag", near_ag[p])
        m2s.append(moved_of(2, g2))
        right = slice(3 * K, NB * K)
        field = fields[p][:, K:] - dot3(split(m2s[p]), split(gram[2, :, right]))
        field = jnp.concatenate([field[:, :K], field], axis=1)
        u = {}
        far_rs.append(rs_start(f"s0f{p}_", [corrected(field, l, u) for l in (3, 4, 5)]))
    q = partial(whole(m01s))
    totals, ys = far_reduce(0, far_rs)
    hn_total = rs_finish("hn_", hn_rs)
    hn_ag = ag_start("hn_ag", [hn_total[i] for i in range(3)])
    project_bases(0, 1)
    subs, far_ags = far_gather(0, totals, ys)
    project_bases(1, 4)
    hn = ag_finish("hn_ag", hn_ag)
    for i, pair in enumerate([(3, 2), (4, 2), (5, 2)]):
        h[pair] = split(hn[i])

    for k in range(ROUNDS):
        zs = [sub_finish(k, p, subs[p]) for p in parts]
        qs, moves = [], []
        for p in parts:
            if k:
                m2 = moved_of(2, ag_finish(f"s{k}n{p}_ag", near_ag[p])[0])
            else:
                m2 = m2s[p]
            g3, g4 = ag_finish(f"s{k}f{p}_ag", far_ags[p])
            moves.append(jnp.concatenate([m2, moved_of(3, g3), moved_of(4, g4)], axis=1))
            qs.append(part(q, p) + composed(cols(0, NF - 1), moves[p]))
        moved = whole(moves)
        step = b["x1"][...] - expand(bhi, blo, cols(2, NL), moved)
        if k == 0:
            out_ref[...] = step
        else:
            out_ref[...] += step

        nb = NB if k + 1 < ROUNDS else NL
        mixes, started = [], []
        for p in parts:
            (mixed,) = ag_finish(f"s{k}_zall{p}", zs[p])
            mixes.append(mixed)
            qs[p] = qs[p] - composed(cols(NF - 1), mixed)
            started.append(level_start(k + 1, p, qs[p]))
        carry(moved, whole(mixes), k + 1 < ROUNDS)
        m01s, near_rs, far_rs = [], [], []
        for p in parts:
            m01, field = level_finish(k + 1, p, qs[p], nb, started[p])
            m01s.append(m01)
            u = {}
            near_rs.append(rs_start(f"s{k + 1}n{p}_", [corrected(field, 2, u)]))
            far_rs.append(rs_start(f"s{k + 1}f{p}_", [corrected(field, l, u) for l in range(3, nb)]))
        m01 = whole(m01s)
        if k + 1 < ROUNDS:
            q = partial(m01)
        else:
            out_ref[...] += b["x"][...] - expand(bhi, blo, cols(0, 2), m01)
        totals, ys = far_reduce(k + 1, far_rs)
        near_ag = [ag_start(f"s{k + 1}n{p}_ag", [rs_finish(f"s{k + 1}n{p}_", near_rs[p])[0]]) for p in parts]
        subs, far_ags = far_gather(k + 1, totals, ys)

    moves = []
    for p in parts:
        g2 = ag_finish(f"s{ROUNDS}n{p}_ag", near_ag[p])[0]
        g3, g4 = ag_finish(f"s{ROUNDS}f{p}_ag", far_ags[p])
        moves.append(
            jnp.concatenate([moved_of(l, g) for l, g in ((2, g2), (3, g3), (4, g4))], axis=1)
        )
    out_ref[...] -= expand(bhi, blo, cols(2, NL), whole(moves))

    for copy in sent:
        copy.wait_send()


def body(rhs, leaf_block, leaf_inverse, level_basis, level_core, skeleton_basis, coupling):
    hbm = pl.BlockSpec(memory_space=pl.ANY)
    out = pl.pallas_call(
        kernel,
        out_shape=jax.ShapeDtypeStruct((M, R), F32),
        in_specs=[hbm] * 7,
        out_specs=pl.BlockSpec(memory_space=pltpu.VMEM),
        scratch_shapes=[
            *SCRATCH.values(),
            pltpu.SemaphoreType.DMA((NSEM,)),
            pltpu.SemaphoreType.DMA((NSEM,)),
        ],
        compiler_params=pltpu.CompilerParams(
            collective_id=0, has_side_effects=True, vmem_limit_bytes=56 * 2**20
        ),
        cost_estimate=pl.CostEstimate(flops=8 * 10**9, bytes_accessed=10 * 10**6, transcendentals=0),
        name="ridge_rounds",
    )(
        rhs[0, 0],
        leaf_block[0, 0],
        leaf_inverse[0, 0],
        level_basis[0, 0],
        level_core[0, 0],
        skeleton_basis[0, 0],
        coupling[0],
    )
    return out[None, None]


def solution(mesh):
    return jax.shard_map(
        body,
        mesh=mesh,
        in_specs=(
            P("sub", "leaf", None, None),
            P("sub", "leaf", None, None),
            P("sub", "leaf", None, None),
            P("sub", "leaf", None, None, None),
            P("sub", "leaf", None, None, None),
            P("sub", "leaf", None, None),
            P("sub", None, None, None),
        ),
        out_specs=P("sub", "leaf", None, None),
        check_vma=False,
    )
```

```python
import jax
import jax.numpy as jnp
from jax import lax
from jax.experimental import pallas as pl
from jax.experimental.pallas import tpu as pltpu
from jax.sharding import PartitionSpec as P

ROUNDS = 2
F32, BF16 = jnp.float32, jnp.bfloat16
M, K, R = 1024, 128, 128
NL = 5
NB = NL + 1
NF = NL - 2 + 1
NZ, NY, NSUB = 8, 4, 8
NH = 1
RH = R // NH
MESH = pl.DeviceIdType.MESH
NN = (((1,), (0,)), ((), ()))
NT = (((1,), (1,)), ((), ()))
TN = (((0,), (0,)), ((), ()))


def split(x):
    hi = x.astype(BF16)
    return hi, (x - hi.astype(F32)).astype(BF16)


def dot(a, b, dims=NN):
    return lax.dot_general(a, b, dims, preferred_element_type=F32)


def dot3(a, b, dims=NN):
    (ah, al), (bh, bl) = a, b
    return dot(ah, bh, dims) + (dot(ah, bl, dims) + dot(al, bh, dims))


def cols(first, last=None):
    return slice(first * K, (first + 1 if last is None else last) * K)


def buffers():
    out = {
        "inv": pltpu.VMEM((M, M), BF16),
        "blk": pltpu.VMEM((M, M), BF16),
        "res": pltpu.VMEM((M, R), F32),
        "bas": pltpu.VMEM((NB, M, K), F32),
        "core": pltpu.VMEM((NL, K, K), F32),
        "coup": pltpu.VMEM((NSUB, K, K), F32),
        "bhi": pltpu.VMEM((M, NB * K), BF16),
        "blo": pltpu.VMEM((M, NB * K), BF16),
        "dhi": pltpu.VMEM((M, NF * K), BF16),
        "dlo": pltpu.VMEM((M, NF * K), BF16),
        "vhi": pltpu.VMEM((M, NF * K), BF16),
        "vlo": pltpu.VMEM((M, NF * K), BF16),
        "ehi": pltpu.VMEM((NF * K, NB * K), BF16),
        "elo": pltpu.VMEM((NF * K, NB * K), BF16),
        "gram": pltpu.VMEM((NL, K, NB * K), F32),
        "chi": pltpu.VMEM((K, NSUB * K), BF16),
        "clo": pltpu.VMEM((K, NSUB * K), BF16),
        "xcat": pltpu.VMEM((M, 2 * R), BF16),
        "x": pltpu.VMEM((M, R), F32),
        "x1": pltpu.VMEM((M, R), F32),
        "h10": pltpu.VMEM((2, K, K), F32),
        "loads": pltpu.SemaphoreType.DMA((NB + 5,)),
    }

    def ring(tag, near, far, back, blk):
        out[tag + "rs_out"] = pltpu.VMEM((NZ, near + far, blk, K), F32)
        out[tag + "rs_in"] = pltpu.VMEM((NZ - 1, near + far, blk, K), F32)
        if far:
            out[tag + "y_out"] = pltpu.VMEM((far, blk, K), F32)
            out[tag + "y_in"] = pltpu.VMEM((NY - 1, far, blk, K), F32)
        out[tag + "ag"] = pltpu.VMEM((NZ, near + back, blk, K), F32)

    ring("hf_", 0, 3, 3, K // NZ)
    ring("hn_", 3, 0, 0, K // NZ)
    out["e_out"] = pltpu.VMEM((2, K, K), F32)
    out["e_quad"] = pltpu.VMEM((3, K, K), F32)
    out["e_pair"] = pltpu.VMEM((K, K), F32)
    for k in range(ROUNDS + 1):
        for p in range(NH):
            ring(f"s{k}n{p}_", 1, 0, 0, RH // NZ)
            ring(f"s{k}f{p}_", 0, 3 if k < ROUNDS else 2, 2, RH // NZ)
            out[f"s{k}_quad_out{p}"] = pltpu.VMEM((2, RH, K), F32)
            out[f"s{k}_quad_in{p}"] = pltpu.VMEM((3, RH, K), F32)
            out[f"s{k}_pair_in{p}"] = pltpu.VMEM((RH, K), F32)
            if k < ROUNDS:
                out[f"s{k}_yall{p}"] = pltpu.VMEM((NSUB, RH // NZ, K), F32)
                out[f"s{k}_zall{p}"] = pltpu.VMEM((NZ, 1, RH // NZ, K), F32)
    return out


NSEM = 160 + 140 * NH
SCRATCH = buffers()


def kernel(rhs_h, blk_h, inv_h, bas_h, core_h, skel_h, coup_h, out_ref, *scratch):
    names = list(SCRATCH)
    b = dict(zip(names, scratch[: len(names)]))
    send_sems, recv_sems = scratch[len(names) :]

    loads = [(bas_h.at[l], b["bas"].at[l]) for l in range(NL)] + [
        (skel_h, b["bas"].at[NL]),
        (core_h, b["core"]),
        (rhs_h, b["res"]),
        (inv_h, b["inv"]),
        (blk_h, b["blk"]),
        (coup_h, b["coup"]),
    ]
    loads = [pltpu.make_async_copy(s, d, b["loads"].at[i]) for i, (s, d) in enumerate(loads)]
    for copy in loads[: NB + 1]:
        copy.start()
    l_core, l_rhs, l_inv, l_blk, l_coup = loads[NB:]

    leaf, sub = lax.axis_index("leaf"), lax.axis_index("sub")
    y, z = lax.div(leaf, NZ), lax.rem(leaf, NZ)
    row = y * NZ
    quad = row + lax.div(z, 4) * 4
    z_peers = [row + lax.rem(z + NZ - d, NZ) for d in range(1, NZ)]
    quad_peers = [quad + lax.rem(z + 4 - d, 4) for d in range(1, 4)]
    pair_peer = leaf + 1 - 2 * lax.rem(z, 2)
    y_peers = [(y + 1 - 2 * lax.rem(y, 2)) * NZ + z, lax.rem(y + 2, NY) * NZ + z, (NY - 1 - y) * NZ + z]
    sub_peers = [lax.rem(sub + NSUB - d, NSUB) for d in range(1, NSUB)]

    barrier = pltpu.get_barrier_semaphore()
    for peer in z_peers + y_peers:
        pl.semaphore_signal(barrier, inc=1, device_id={"leaf": peer}, device_id_type=MESH)
    for peer in sub_peers:
        pl.semaphore_signal(barrier, inc=1, device_id={"sub": peer}, device_id_type=MESH)

    sent = []

    def send(src, dst, where):
        i = len(sent)
        copy = pltpu.make_async_remote_copy(
            src_ref=src,
            dst_ref=dst,
            send_sem=send_sems.at[i],
            recv_sem=recv_sems.at[i],
            device_id=where,
            device_id_type=MESH,
        )
        copy.start()
        sent.append(copy)
        return copy

    def wait(copies):
        for copy in copies:
            copy.wait_recv()

    far_first = [3, 2, 4, 1, 5, 0, 6]

    def rs_store(tag, mats):
        for m, mat in enumerate(mats):
            b[tag + "rs_out"][:, m] = mat.reshape(NZ, mat.shape[0] // NZ, K)

    def rs_start(tag, mats):
        rs_store(tag, mats)
        out = b[tag + "rs_out"]
        return [
            send(out.at[lax.rem(z + NZ - d - 1, NZ)], b[tag + "rs_in"].at[d], {"leaf": z_peers[d]})
            for d in far_first
        ]

    def rs_finish(tag, copies):
        wait(copies)
        total = b[tag + "rs_out"][z]
        for d in range(NZ - 1):
            total = total + b[tag + "rs_in"][d]
        return total

    def y_start(tag, total, two):
        n = total.shape[0]
        y_out, y_in = b[tag + "y_out"], b[tag + "y_in"]
        y_out[...] = total
        return [
            send(y_out.at[pl.ds(f, n - f)], y_in.at[e, pl.ds(f, n - f)], {"leaf": y_peers[e]})
            for e, f in ((1, two), (2, two), (0, 0))
            if n > f
        ]

    def y_finish(tag, total, two, copies):
        wait(copies)
        y_in = b[tag + "y_in"]
        parts = [total[i] + y_in[0, i] for i in range(two)]
        parts += [(total[i] + y_in[0, i]) + (y_in[1, i] + y_in[2, i]) for i in range(two, total.shape[0])]
        return parts

    def ag_start(name, blocks):
        ref = b[name]
        for i, block in enumerate(blocks):
            ref[z, i] = block
        return [send(ref.at[z], ref.at[z], {"leaf": z_peers[d]}) for d in far_first]

    def ag_finish(name, copies):
        wait(copies)
        ref = b[name]
        return [ref[:, i].reshape(NZ * ref.shape[2], K) for i in range(ref.shape[1])]

    bhi, blo, gram = b["bhi"], b["blo"], b["gram"]

    for l in range(NB):
        loads[l].wait()
        bhi[:, cols(l)], blo[:, cols(l)] = split(b["bas"][l])
    l_inv.start()
    l_rhs.start()
    for j in range(NL):
        right = slice((j + 1) * K, NB * K)
        here_hi, here_lo = bhi[:, cols(j)], blo[:, cols(j)]
        gram[j, :, right] = dot(here_hi, bhi[:, right], TN) + (
            dot(here_hi, blo[:, right], TN) + dot(here_lo, bhi[:, right], TN)
        )
    l_blk.start()
    l_coup.start()
    l_core.wait()
    core = [split(b["core"][l]) for l in range(NL)]

    def coupled(l, j):
        return dot3(core[j], split(gram[j, :, cols(l)]), TN)

    b["h10"][0] = coupled(1, 0)
    hf_mats = [coupled(4, 3), coupled(5, 3), coupled(5, 4)]
    pl.semaphore_wait(barrier, len(z_peers) + len(y_peers) + len(sub_peers))
    h10_copy = send(b["h10"].at[0], b["h10"].at[1], {"leaf": pair_peer})
    hf_rs = rs_start("hf_", hf_mats)

    def spread(value):
        b["xcat"][:, :R], b["xcat"][:, R:] = split(value)

    def leaf_product(mat, finish):
        @pl.loop(0, M // 256)
        def _(t):
            rows = pl.ds(pl.multiple_of(t * 256, 256), 256)
            both = dot(mat[rows, :], b["xcat"][...])
            finish(rows, both[:, :R] + both[:, R:])

    def put_x(rows, value):
        b["x"][rows, :] = value

    def reduce_res(rows, value):
        b["res"][rows, :] -= value

    def project():
        hi, lo = split(b["x"][...].T)
        both = dot(jnp.concatenate([hi, lo], axis=0), bhi[...])
        return both[:R] + both[R:] + dot(hi, blo[...])

    def expand(high, low, where, moved):
        hi, lo = split(moved)
        both = dot(high[:, where], jnp.concatenate([hi, lo], axis=0), NT)
        return both[:, :R] + both[:, R:] + dot(low[:, where], hi, NT)

    def composed(where, moved):
        hi, lo = split(moved)
        both = dot(jnp.concatenate([hi, lo], axis=0), b["ehi"][where, :])
        return both[: moved.shape[0]] + both[moved.shape[0] :] + dot(hi, b["elo"][where, :])

    def block_bases():
        @pl.loop(0, M // 256)
        def _(t):
            rows = pl.ds(pl.multiple_of(t * 256, 256), 256)
            some = cols(2, NL)
            value = dot(b["blk"][rows, :], bhi[:, some]) + dot(b["blk"][rows, :], blo[:, some])
            b["dhi"][rows, cols(0, NF - 1)], b["dlo"][rows, cols(0, NF - 1)] = split(value)

        b["dhi"][:, cols(NF - 1)] = bhi[:, cols(NL)]
        b["dlo"][:, cols(NF - 1)] = blo[:, cols(NL)]

    def inverse_bases(first, last):
        @pl.loop(first, last)
        def _(t):
            rows = pl.ds(pl.multiple_of(t * 256, 256), 256)
            value = dot(b["inv"][rows, :], b["dhi"][...]) + dot(b["inv"][rows, :], b["dlo"][...])
            b["vhi"][rows, :], b["vlo"][rows, :] = split(value)

    def project_bases(first, last):
        for c in range(first, last):
            hi, lo = b["vhi"][:, cols(c)], b["vlo"][:, cols(c)]
            value = dot(hi, bhi[...], TN) + (dot(hi, blo[...], TN) + dot(lo, bhi[...], TN))
            b["ehi"][cols(c), :], b["elo"][cols(c), :] = split(value)

    h = {}

    def level_start(k, p, q):
        u0 = q[:, cols(0)]
        u1 = q[:, cols(1)] - dot3(split(u0), h[1, 0])
        out = b[f"s{k}_quad_out{p}"]
        out[1] = u1
        out[0] = u0
        copies = [
            send(out.at[1], b[f"s{k}_quad_in{p}"].at[d], {"leaf": quad_peers[d]}) for d in (1, 2, 0)
        ]
        return u0, u1, copies + [send(out.at[0], b[f"s{k}_pair_in{p}"], {"leaf": pair_peer})]

    def level_finish(k, p, q, nb, started, late=None):
        u0, u1, copies = started
        wait(copies)
        quad_in = b[f"s{k}_quad_in{p}"]
        g0 = u0 + b[f"s{k}_pair_in{p}"][...]
        g1 = (u1 + quad_in[0]) + (quad_in[1] + quad_in[2])
        if late is not None:
            g0, g1 = g0 - late[:, cols(0)], g1 - late[:, cols(1)]
        m01 = jnp.concatenate([dot3(split(g0), core[0], NT), dot3(split(g1), core[1], NT)], axis=1)
        right = slice(2 * K, nb * K)
        both = jnp.concatenate([gram[0, :, right], gram[1, :, right]], axis=0)
        return m01, q[:, right] - dot3(split(m01), split(both))

    def corrected(field, l, u):
        ul = field[:, cols(l - 2)]
        for j in sorted(u):
            ul = ul - dot3(u[j], h[l, j])
        u[l] = split(ul)
        return ul

    def partial(m01):
        x1 = b["x"][...] - expand(bhi, blo, cols(0, 2), m01)
        b["x1"][...] = x1
        spread(x1)
        leaf_product(b["blk"], reduce_res)
        spread(b["res"][...])
        leaf_product(b["inv"], put_x)
        return project()

    def moved_of(level, g):
        return dot3(split(g), core[level], NT)

    def sub_start(k, p, block):
        yall = b[f"s{k}_yall{p}"]
        yall[sub] = block
        return [send(yall.at[sub], yall.at[sub], {"sub": peer}) for peer in sub_peers]

    def sub_finish(k, p, copies):
        wait(copies)
        yall = b[f"s{k}_yall{p}"]
        hi, lo = split(jnp.concatenate([yall[t] for t in range(NSUB)], axis=1))
        if NH == 1:
            both = dot(jnp.concatenate([hi, lo], axis=0), b["chi"][...], NT)
            value = both[: RH // NZ] + both[RH // NZ :] + dot(hi, b["clo"][...], NT)
        else:
            value = dot(hi, b["chi"][...], NT) + (dot(lo, b["chi"][...], NT) + dot(hi, b["clo"][...], NT))
        return ag_start(f"s{k}_zall{p}", [value])

    def carry(moved, mixed, further):
        all_moved = jnp.concatenate([moved, -mixed], axis=1)
        b["x"][...] += expand(b["vhi"], b["vlo"], cols(0, NF), all_moved)
        if further:
            b["res"][...] += expand(b["dhi"], b["dlo"], cols(0, NF), all_moved)

    parts = range(NH)

    def part(value, p):
        return value[p * RH : (p + 1) * RH]

    def whole(values):
        return jnp.concatenate(list(values), axis=0)

    def far_reduce(k, rs):
        totals = [None] * NH
        ys = [None] * NH
        for p in parts:
            totals[p] = rs_finish(f"s{k}f{p}_", rs[p])
            ys[p] = y_start(f"s{k}f{p}_", totals[p], 1)
        return totals, ys

    def far_gather(k, totals, ys):
        subs, ags = [None] * NH, [None] * NH
        for p in parts:
            sums = y_finish(f"s{k}f{p}_", totals[p], 1, ys[p])
            if k < ROUNDS:
                subs[p] = sub_start(k, p, sums[2])
            ags[p] = ag_start(f"s{k}f{p}_ag", sums[:2])
        return subs, ags

    l_rhs.wait()
    l_inv.wait()
    spread(b["res"][...])
    leaf_product(b["inv"], put_x)
    q = project()
    wait([h10_copy])
    h[1, 0] = split(b["h10"][0] + b["h10"][1])
    q = [part(q, p) for p in parts]
    started = [level_start(0, p, q[p]) for p in parts]
    rs_store("hn_", [coupled(3, 2), coupled(4, 2), coupled(5, 2)])
    l_blk.wait()
    block_bases()
    l_coup.wait()
    for t in range(NSUB):
        b["chi"][:, cols(t)], b["clo"][:, cols(t)] = split(b["coup"][t])
    hf_total = rs_finish("hf_", hf_rs)
    hf_y = y_start("hf_", hf_total, 2)
    fields, m01s, near_rs = [], [], []
    for p in parts:
        m01, field = level_finish(0, p, q[p], NB, started[p])
        m01s.append(m01)
        fields.append(field)
        near_rs.append(rs_start(f"s0n{p}_", [field[:, cols(0)]]))
    hf_ag = ag_start("hf_ag", y_finish("hf_", hf_total, 2, hf_y))
    inverse_bases(0, 3)
    near_ag = [ag_start(f"s0n{p}_ag", [rs_finish(f"s0n{p}_", near_rs[p])[0]]) for p in parts]
    hn_rs = rs_start("hn_", [])
    inverse_bases(3, 4)
    project_bases(NF - 1, NF)
    skel = cols(NF - 1)
    e0 = b["ehi"][skel, cols(0)], b["elo"][skel, cols(0)]
    e_out = b["e_out"]
    e_out[0] = e0[0].astype(F32) + e0[1].astype(F32)
    e_out[1] = b["ehi"][skel, cols(1)].astype(F32) + b["elo"][skel, cols(1)].astype(F32) - dot3(e0, h[1, 0])
    hf = ag_finish("hf_ag", hf_ag)
    for i, pair in enumerate([(4, 3), (5, 3), (5, 4)]):
        h[pair] = split(hf[i])
    m2s, far_rs = [], []
    for p in parts:
        (g2,) = ag_finish(f"s0n{p}_ag", near_ag[p])
        m2s.append(moved_of(2, g2))
        right = slice(3 * K, NB * K)
        field = fields[p][:, K:] - dot3(split(m2s[p]), split(gram[2, :, right]))
        field = jnp.concatenate([field[:, :K], field], axis=1)
        u = {}
        far_rs.append(rs_start(f"s0f{p}_", [corrected(field, l, u) for l in (3, 4, 5)]))
    q = partial(whole(m01s))
    totals, ys = far_reduce(0, far_rs)
    hn_total = rs_finish("hn_", hn_rs)
    hn_ag = ag_start("hn_ag", [hn_total[i] for i in range(3)])
    e_copies = [send(e_out.at[1], b["e_quad"].at[d], {"leaf": quad_peers[d]}) for d in (1, 2, 0)]
    e_copies.append(send(e_out.at[0], b["e_pair"], {"leaf": pair_peer}))
    project_bases(0, 1)
    subs, far_ags = far_gather(0, totals, ys)
    project_bases(1, NF - 1)
    hn = ag_finish("hn_ag", hn_ag)
    for i, pair in enumerate([(3, 2), (4, 2), (5, 2)]):
        h[pair] = split(hn[i])

    for k in range(ROUNDS):
        zs = [sub_finish(k, p, subs[p]) for p in parts]
        qs, moves = [], []
        for p in parts:
            if k:
                m2 = moved_of(2, ag_finish(f"s{k}n{p}_ag", near_ag[p])[0])
            else:
                m2 = m2s[p]
            g3, g4 = ag_finish(f"s{k}f{p}_ag", far_ags[p])
            moves.append(jnp.concatenate([m2, moved_of(3, g3), moved_of(4, g4)], axis=1))
            qs.append(part(q, p) + composed(cols(0, NF - 1), moves[p]))
        nb = NB if k + 1 < ROUNDS else NL
        started = [level_start(k + 1, p, qs[p]) for p in parts]
        moved = whole(moves)
        step = b["x1"][...] - expand(bhi, blo, cols(2, NL), moved)
        if k == 0:
            out_ref[...] = step
            wait(e_copies)
            e_quad = b["e_quad"]
            shared = split(
                jnp.concatenate(
                    [e_out[0] + b["e_pair"][...], (e_out[1] + e_quad[0]) + (e_quad[1] + e_quad[2])], axis=1
                )
            )
        else:
            out_ref[...] += step
        mixes, lates = [], []
        for p in parts:
            (mixed,) = ag_finish(f"s{k}_zall{p}", zs[p])
            mixes.append(mixed)
            qs[p] = qs[p] - composed(cols(NF - 1), mixed)
            lates.append(dot3(split(mixed), shared))
        carry(moved, whole(mixes), k + 1 < ROUNDS)
        m01s, near_rs, far_rs = [], [], []
        for p in parts:
            m01, field = level_finish(k + 1, p, qs[p], nb, started[p], lates[p])
            m01s.append(m01)
            u = {}
            near_rs.append(rs_start(f"s{k + 1}n{p}_", [corrected(field, 2, u)]))
            far_rs.append(rs_start(f"s{k + 1}f{p}_", [corrected(field, l, u) for l in range(3, nb)]))
        m01 = whole(m01s)
        if k + 1 < ROUNDS:
            q = partial(m01)
        else:
            out_ref[...] += b["x"][...] - expand(bhi, blo, cols(0, 2), m01)
        totals, ys = far_reduce(k + 1, far_rs)
        near_ag = [ag_start(f"s{k + 1}n{p}_ag", [rs_finish(f"s{k + 1}n{p}_", near_rs[p])[0]]) for p in parts]
        subs, far_ags = far_gather(k + 1, totals, ys)

    moves = []
    for p in parts:
        g2 = ag_finish(f"s{ROUNDS}n{p}_ag", near_ag[p])[0]
        g3, g4 = ag_finish(f"s{ROUNDS}f{p}_ag", far_ags[p])
        moves.append(
            jnp.concatenate([moved_of(l, g) for l, g in ((2, g2), (3, g3), (4, g4))], axis=1)
        )
    out_ref[...] -= expand(bhi, blo, cols(2, NL), whole(moves))

    for copy in sent:
        copy.wait_send()


def body(rhs, leaf_block, leaf_inverse, level_basis, level_core, skeleton_basis, coupling):
    hbm = pl.BlockSpec(memory_space=pl.ANY)
    out = pl.pallas_call(
        kernel,
        out_shape=jax.ShapeDtypeStruct((M, R), F32),
        in_specs=[hbm] * 7,
        out_specs=pl.BlockSpec(memory_space=pltpu.VMEM),
        scratch_shapes=[
            *SCRATCH.values(),
            pltpu.SemaphoreType.DMA((NSEM,)),
            pltpu.SemaphoreType.DMA((NSEM,)),
        ],
        compiler_params=pltpu.CompilerParams(
            collective_id=0, has_side_effects=True, vmem_limit_bytes=56 * 2**20
        ),
        cost_estimate=pl.CostEstimate(flops=8 * 10**9, bytes_accessed=10 * 10**6, transcendentals=0),
        name="ridge_rounds",
    )(
        rhs[0, 0],
        leaf_block[0, 0],
        leaf_inverse[0, 0],
        level_basis[0, 0],
        level_core[0, 0],
        skeleton_basis[0, 0],
        coupling[0],
    )
    return out[None, None]


def solution(mesh):
    return jax.shard_map(
        body,
        mesh=mesh,
        in_specs=(
            P("sub", "leaf", None, None),
            P("sub", "leaf", None, None),
            P("sub", "leaf", None, None),
            P("sub", "leaf", None, None, None),
            P("sub", "leaf", None, None, None),
            P("sub", "leaf", None, None),
            P("sub", None, None, None),
        ),
        out_specs=P("sub", "leaf", None, None),
        check_vma=False,
    )
```

```python
import jax
import jax.numpy as jnp
from jax import lax
from jax.experimental import pallas as pl
from jax.experimental.pallas import tpu as pltpu
from jax.sharding import PartitionSpec as P

ROUNDS = 2
F32, BF16 = jnp.float32, jnp.bfloat16
M, K, R = 1024, 128, 128
NL = 5
NB = NL + 1
NF = NL - 2 + 1
NZ, NY, NSUB = 8, 4, 8
NH = 1
RH = R // NH
MESH = pl.DeviceIdType.MESH
NN = (((1,), (0,)), ((), ()))
NT = (((1,), (1,)), ((), ()))
TN = (((0,), (0,)), ((), ()))


def split(x):
    hi = x.astype(BF16)
    return hi, (x - hi.astype(F32)).astype(BF16)


def dot(a, b, dims=NN):
    return lax.dot_general(a, b, dims, preferred_element_type=F32)


def dot3(a, b, dims=NN):
    (ah, al), (bh, bl) = a, b
    return dot(ah, bh, dims) + (dot(ah, bl, dims) + dot(al, bh, dims))


def cols(first, last=None):
    return slice(first * K, (first + 1 if last is None else last) * K)


def buffers():
    out = {
        "inv": pltpu.VMEM((M, M), BF16),
        "blk": pltpu.VMEM((M, M), BF16),
        "res": pltpu.VMEM((M, R), F32),
        "bas": pltpu.VMEM((NB, M, K), F32),
        "core": pltpu.VMEM((NL, K, K), F32),
        "coup": pltpu.VMEM((NSUB, K, K), F32),
        "bhi": pltpu.VMEM((M, NB * K), BF16),
        "blo": pltpu.VMEM((M, NB * K), BF16),
        "dhi": pltpu.VMEM((M, NF * K), BF16),
        "dlo": pltpu.VMEM((M, NF * K), BF16),
        "vhi": pltpu.VMEM((M, NF * K), BF16),
        "vlo": pltpu.VMEM((M, NF * K), BF16),
        "ehi": pltpu.VMEM((NF * K, NB * K), BF16),
        "elo": pltpu.VMEM((NF * K, NB * K), BF16),
        "gram": pltpu.VMEM((NL, K, NB * K), F32),
        "chi": pltpu.VMEM((K, NSUB * K), BF16),
        "clo": pltpu.VMEM((K, NSUB * K), BF16),
        "xcat": pltpu.VMEM((M, 2 * R), BF16),
        "x": pltpu.VMEM((M, R), F32),
        "x1": pltpu.VMEM((M, R), F32),
        "h10": pltpu.VMEM((2, K, K), F32),
        "loads": pltpu.SemaphoreType.DMA((NB + 5,)),
    }

    def ring(tag, near, far, back, blk):
        out[tag + "rs_out"] = pltpu.VMEM((NZ, near + far, blk, K), F32)
        out[tag + "rs_in"] = pltpu.VMEM((NZ - 1, near + far, blk, K), F32)
        if far:
            out[tag + "y_out"] = pltpu.VMEM((far, blk, K), F32)
            out[tag + "y_in"] = pltpu.VMEM((NY - 1, far, blk, K), F32)
        out[tag + "ag"] = pltpu.VMEM((NZ, near + back, blk, K), F32)

    ring("hf_", 0, 3, 3, K // NZ)
    ring("hn_", 3, 0, 0, K // NZ)
    for k in range(ROUNDS + 1):
        for p in range(NH):
            ring(f"s{k}n{p}_", 1, 0, 0, RH // NZ)
            ring(f"s{k}f{p}_", 0, 3 if k < ROUNDS else 2, 2, RH // NZ)
            out[f"s{k}_quad_out{p}"] = pltpu.VMEM((2, RH, K), F32)
            out[f"s{k}_quad_in{p}"] = pltpu.VMEM((3, RH, K), F32)
            out[f"s{k}_pair_in{p}"] = pltpu.VMEM((RH, K), F32)
            if k < ROUNDS:
                out[f"s{k}_yall{p}"] = pltpu.VMEM((NSUB, RH // NZ, K), F32)
                out[f"s{k}_zall{p}"] = pltpu.VMEM((NZ, 1, RH // NZ, K), F32)
    return out


NSEM = 160 + 140 * NH
SCRATCH = buffers()


def kernel(rhs_h, blk_h, inv_h, bas_h, core_h, skel_h, coup_h, out_ref, *scratch):
    names = list(SCRATCH)
    b = dict(zip(names, scratch[: len(names)]))
    send_sems, recv_sems = scratch[len(names) :]

    loads = [(bas_h.at[l], b["bas"].at[l]) for l in range(NL)] + [
        (skel_h, b["bas"].at[NL]),
        (core_h, b["core"]),
        (rhs_h, b["res"]),
        (inv_h, b["inv"]),
        (blk_h, b["blk"]),
        (coup_h, b["coup"]),
    ]
    loads = [pltpu.make_async_copy(s, d, b["loads"].at[i]) for i, (s, d) in enumerate(loads)]
    for copy in loads[: NB + 1]:
        copy.start()
    l_core, l_rhs, l_inv, l_blk, l_coup = loads[NB:]

    leaf, sub = lax.axis_index("leaf"), lax.axis_index("sub")
    y, z = lax.div(leaf, NZ), lax.rem(leaf, NZ)
    row = y * NZ
    quad = row + lax.div(z, 4) * 4
    z_peers = [row + lax.rem(z + NZ - d, NZ) for d in range(1, NZ)]
    quad_peers = [quad + lax.rem(z + 4 - d, 4) for d in range(1, 4)]
    pair_peer = leaf + 1 - 2 * lax.rem(z, 2)
    y_peers = [(y + 1 - 2 * lax.rem(y, 2)) * NZ + z, lax.rem(y + 2, NY) * NZ + z, (NY - 1 - y) * NZ + z]
    sub_peers = [lax.rem(sub + NSUB - d, NSUB) for d in range(1, NSUB)]

    barrier = pltpu.get_barrier_semaphore()
    for peer in z_peers + y_peers:
        pl.semaphore_signal(barrier, inc=1, device_id={"leaf": peer}, device_id_type=MESH)
    for peer in sub_peers:
        pl.semaphore_signal(barrier, inc=1, device_id={"sub": peer}, device_id_type=MESH)

    sent = []

    def send(src, dst, where):
        i = len(sent)
        copy = pltpu.make_async_remote_copy(
            src_ref=src,
            dst_ref=dst,
            send_sem=send_sems.at[i],
            recv_sem=recv_sems.at[i],
            device_id=where,
            device_id_type=MESH,
        )
        copy.start()
        sent.append(copy)
        return copy

    def wait(copies):
        for copy in copies:
            copy.wait_recv()

    drained = []

    def drain(recent):
        for copy in sent[len(drained) : len(sent) - recent]:
            copy.wait_send()
            drained.append(copy)

    far_first = [3, 2, 4, 1, 5, 0, 6]

    def rs_store(tag, mats):
        for m, mat in enumerate(mats):
            b[tag + "rs_out"][:, m] = mat.reshape(NZ, mat.shape[0] // NZ, K)

    def rs_start(tag, mats):
        rs_store(tag, mats)
        out = b[tag + "rs_out"]
        return [
            send(out.at[lax.rem(z + NZ - d - 1, NZ)], b[tag + "rs_in"].at[d], {"leaf": z_peers[d]})
            for d in far_first
        ]

    def rs_finish(tag, copies):
        wait(copies)
        total = b[tag + "rs_out"][z]
        for d in range(NZ - 1):
            total = total + b[tag + "rs_in"][d]
        return total

    def y_start(tag, total, two):
        n = total.shape[0]
        y_out, y_in = b[tag + "y_out"], b[tag + "y_in"]
        y_out[...] = total
        return [
            send(y_out.at[pl.ds(f, n - f)], y_in.at[e, pl.ds(f, n - f)], {"leaf": y_peers[e]})
            for e, f in ((1, two), (2, two), (0, 0))
            if n > f
        ]

    def y_finish(tag, total, two, copies):
        wait(copies)
        y_in = b[tag + "y_in"]
        parts = [total[i] + y_in[0, i] for i in range(two)]
        parts += [(total[i] + y_in[0, i]) + (y_in[1, i] + y_in[2, i]) for i in range(two, total.shape[0])]
        return parts

    def ag_start(name, blocks):
        ref = b[name]
        for i, block in enumerate(blocks):
            ref[z, i] = block
        return [send(ref.at[z], ref.at[z], {"leaf": z_peers[d]}) for d in far_first]

    def ag_finish(name, copies):
        wait(copies)
        ref = b[name]
        return [ref[:, i].reshape(NZ * ref.shape[2], K) for i in range(ref.shape[1])]

    bhi, blo, gram = b["bhi"], b["blo"], b["gram"]

    for l in range(NB):
        loads[l].wait()
        bhi[:, cols(l)], blo[:, cols(l)] = split(b["bas"][l])
    l_inv.start()
    l_rhs.start()
    for j in range(NL):
        right = slice((j + 1) * K, NB * K)
        here_hi, here_lo = bhi[:, cols(j)], blo[:, cols(j)]
        gram[j, :, right] = dot(here_hi, bhi[:, right], TN) + (
            dot(here_hi, blo[:, right], TN) + dot(here_lo, bhi[:, right], TN)
        )
    l_blk.start()
    l_coup.start()
    l_core.wait()
    core = [split(b["core"][l]) for l in range(NL)]

    def coupled(l, j):
        return dot3(core[j], split(gram[j, :, cols(l)]), TN)

    b["h10"][0] = coupled(1, 0)
    hf_mats = [coupled(4, 3), coupled(5, 3), coupled(5, 4)]
    pl.semaphore_wait(barrier, len(z_peers) + len(y_peers) + len(sub_peers))
    h10_copy = send(b["h10"].at[0], b["h10"].at[1], {"leaf": pair_peer})
    hf_rs = rs_start("hf_", hf_mats)

    def spread(value):
        b["xcat"][:, :R], b["xcat"][:, R:] = split(value)

    def leaf_product(mat, finish):
        @pl.loop(0, M // 256)
        def _(t):
            rows = pl.ds(pl.multiple_of(t * 256, 256), 256)
            both = dot(mat[rows, :], b["xcat"][...])
            finish(rows, both[:, :R] + both[:, R:])

    def put_x(rows, value):
        b["x"][rows, :] = value

    def reduce_res(rows, value):
        b["res"][rows, :] -= value

    def project():
        hi, lo = split(b["x"][...].T)
        both = dot(jnp.concatenate([hi, lo], axis=0), bhi[...])
        return both[:R] + both[R:] + dot(hi, blo[...])

    def expand(high, low, where, moved):
        hi, lo = split(moved)
        both = dot(high[:, where], jnp.concatenate([hi, lo], axis=0), NT)
        return both[:, :R] + both[:, R:] + dot(low[:, where], hi, NT)

    def composed(where, moved):
        hi, lo = split(moved)
        both = dot(jnp.concatenate([hi, lo], axis=0), b["ehi"][where, :])
        return both[: moved.shape[0]] + both[moved.shape[0] :] + dot(hi, b["elo"][where, :])

    def block_bases():
        @pl.loop(0, M // 256)
        def _(t):
            rows = pl.ds(pl.multiple_of(t * 256, 256), 256)
            some = cols(2, NL)
            value = dot(b["blk"][rows, :], bhi[:, some]) + dot(b["blk"][rows, :], blo[:, some])
            b["dhi"][rows, cols(0, NF - 1)], b["dlo"][rows, cols(0, NF - 1)] = split(value)

        b["dhi"][:, cols(NF - 1)] = bhi[:, cols(NL)]
        b["dlo"][:, cols(NF - 1)] = blo[:, cols(NL)]

    def inverse_bases(first, last):
        @pl.loop(first, last)
        def _(t):
            rows = pl.ds(pl.multiple_of(t * 256, 256), 256)
            value = dot(b["inv"][rows, :], b["dhi"][...]) + dot(b["inv"][rows, :], b["dlo"][...])
            b["vhi"][rows, :], b["vlo"][rows, :] = split(value)

    def project_bases(first, last):
        for c in range(first, last):
            hi, lo = b["vhi"][:, cols(c)], b["vlo"][:, cols(c)]
            value = dot(hi, bhi[...], TN) + (dot(hi, blo[...], TN) + dot(lo, bhi[...], TN))
            b["ehi"][cols(c), :], b["elo"][cols(c), :] = split(value)

    h = {}

    def level_start(k, p, q):
        u0 = q[:, cols(0)]
        u1 = q[:, cols(1)] - dot3(split(u0), h[1, 0])
        out = b[f"s{k}_quad_out{p}"]
        out[1] = u1
        out[0] = u0
        copies = [
            send(out.at[1], b[f"s{k}_quad_in{p}"].at[d], {"leaf": quad_peers[d]}) for d in (1, 2, 0)
        ]
        return u0, u1, copies + [send(out.at[0], b[f"s{k}_pair_in{p}"], {"leaf": pair_peer})]

    def level_finish(k, p, q, nb, started):
        u0, u1, copies = started
        wait(copies)
        quad_in = b[f"s{k}_quad_in{p}"]
        g0 = u0 + b[f"s{k}_pair_in{p}"][...]
        g1 = (u1 + quad_in[0]) + (quad_in[1] + quad_in[2])
        m01 = jnp.concatenate([dot3(split(g0), core[0], NT), dot3(split(g1), core[1], NT)], axis=1)
        right = slice(2 * K, nb * K)
        both = jnp.concatenate([gram[0, :, right], gram[1, :, right]], axis=0)
        return m01, q[:, right] - dot3(split(m01), split(both))

    def corrected(field, l, u):
        ul = field[:, cols(l - 2)]
        for j in sorted(u):
            ul = ul - dot3(u[j], h[l, j])
        u[l] = split(ul)
        return ul

    def partial(m01):
        x1 = b["x"][...] - expand(bhi, blo, cols(0, 2), m01)
        b["x1"][...] = x1
        spread(x1)
        leaf_product(b["blk"], reduce_res)
        spread(b["res"][...])
        leaf_product(b["inv"], put_x)
        return project()

    def moved_of(level, g):
        return dot3(split(g), core[level], NT)

    def sub_start(k, p, block):
        yall = b[f"s{k}_yall{p}"]
        yall[sub] = block
        return [send(yall.at[sub], yall.at[sub], {"sub": peer}) for peer in sub_peers]

    def sub_finish(k, p, copies):
        wait(copies)
        yall = b[f"s{k}_yall{p}"]
        hi, lo = split(jnp.concatenate([yall[t] for t in range(NSUB)], axis=1))
        if NH == 1:
            both = dot(jnp.concatenate([hi, lo], axis=0), b["chi"][...], NT)
            value = both[: RH // NZ] + both[RH // NZ :] + dot(hi, b["clo"][...], NT)
        else:
            value = dot(hi, b["chi"][...], NT) + (dot(lo, b["chi"][...], NT) + dot(hi, b["clo"][...], NT))
        return ag_start(f"s{k}_zall{p}", [value])

    def carry(moved, mixed, further):
        all_moved = jnp.concatenate([moved, -mixed], axis=1)
        b["x"][...] += expand(b["vhi"], b["vlo"], cols(0, NF), all_moved)
        if further:
            b["res"][...] += expand(b["dhi"], b["dlo"], cols(0, NF), all_moved)

    parts = range(NH)

    def part(value, p):
        return value[p * RH : (p + 1) * RH]

    def whole(values):
        return jnp.concatenate(list(values), axis=0)

    def far_reduce(k, rs):
        drain(14 * NH)
        totals = [None] * NH
        ys = [None] * NH
        for p in parts:
            totals[p] = rs_finish(f"s{k}f{p}_", rs[p])
            ys[p] = y_start(f"s{k}f{p}_", totals[p], 1)
        return totals, ys

    def far_gather(k, totals, ys):
        drain(17 * NH)
        subs, ags = [None] * NH, [None] * NH
        for p in parts:
            sums = y_finish(f"s{k}f{p}_", totals[p], 1, ys[p])
            if k < ROUNDS:
                subs[p] = sub_start(k, p, sums[2])
            ags[p] = ag_start(f"s{k}f{p}_ag", sums[:2])
        return subs, ags

    l_rhs.wait()
    l_inv.wait()
    spread(b["res"][...])
    leaf_product(b["inv"], put_x)
    q = project()
    wait([h10_copy])
    h[1, 0] = split(b["h10"][0] + b["h10"][1])
    q = [part(q, p) for p in parts]
    started = [level_start(0, p, q[p]) for p in parts]
    rs_store("hn_", [coupled(3, 2), coupled(4, 2), coupled(5, 2)])
    l_blk.wait()
    block_bases()
    l_coup.wait()
    for t in range(NSUB):
        b["chi"][:, cols(t)], b["clo"][:, cols(t)] = split(b["coup"][t])
    hf_total = rs_finish("hf_", hf_rs)
    hf_y = y_start("hf_", hf_total, 2)
    fields, m01s, near_rs = [], [], []
    for p in parts:
        m01, field = level_finish(0, p, q[p], NB, started[p])
        m01s.append(m01)
        fields.append(field)
        near_rs.append(rs_start(f"s0n{p}_", [field[:, cols(0)]]))
    hf_ag = ag_start("hf_ag", y_finish("hf_", hf_total, 2, hf_y))
    inverse_bases(0, 3)
    near_ag = [ag_start(f"s0n{p}_ag", [rs_finish(f"s0n{p}_", near_rs[p])[0]]) for p in parts]
    hn_rs = rs_start("hn_", [])
    inverse_bases(3, 4)
    hf = ag_finish("hf_ag", hf_ag)
    for i, pair in enumerate([(4, 3), (5, 3), (5, 4)]):
        h[pair] = split(hf[i])
    m2s, far_rs = [], []
    for p in parts:
        (g2,) = ag_finish(f"s0n{p}_ag", near_ag[p])
        m2s.append(moved_of(2, g2))
        right = slice(3 * K, NB * K)
        field = fields[p][:, K:] - dot3(split(m2s[p]), split(gram[2, :, right]))
        field = jnp.concatenate([field[:, :K], field], axis=1)
        u = {}
        far_rs.append(rs_start(f"s0f{p}_", [corrected(field, l, u) for l in (3, 4, 5)]))
    q = partial(whole(m01s))
    totals, ys = far_reduce(0, far_rs)
    hn_total = rs_finish("hn_", hn_rs)
    hn_ag = ag_start("hn_ag", [hn_total[i] for i in range(3)])
    project_bases(0, 1)
    subs, far_ags = far_gather(0, totals, ys)
    project_bases(1, 4)
    hn = ag_finish("hn_ag", hn_ag)
    for i, pair in enumerate([(3, 2), (4, 2), (5, 2)]):
        h[pair] = split(hn[i])

    for k in range(ROUNDS):
        zs = [sub_finish(k, p, subs[p]) for p in parts]
        qs, moves = [], []
        for p in parts:
            if k:
                m2 = moved_of(2, ag_finish(f"s{k}n{p}_ag", near_ag[p])[0])
            else:
                m2 = m2s[p]
            g3, g4 = ag_finish(f"s{k}f{p}_ag", far_ags[p])
            moves.append(jnp.concatenate([m2, moved_of(3, g3), moved_of(4, g4)], axis=1))
            qs.append(part(q, p) + composed(cols(0, NF - 1), moves[p]))
        moved = whole(moves)
        step = b["x1"][...] - expand(bhi, blo, cols(2, NL), moved)
        if k == 0:
            out_ref[...] = step
        else:
            out_ref[...] += step

        nb = NB if k + 1 < ROUNDS else NL
        mixes, started = [], []
        for p in parts:
            (mixed,) = ag_finish(f"s{k}_zall{p}", zs[p])
            mixes.append(mixed)
            qs[p] = qs[p] - composed(cols(NF - 1), mixed)
            started.append(level_start(k + 1, p, qs[p]))
        carry(moved, whole(mixes), k + 1 < ROUNDS)
        m01s, near_rs, far_rs = [], [], []
        for p in parts:
            m01, field = level_finish(k + 1, p, qs[p], nb, started[p])
            m01s.append(m01)
            u = {}
            near_rs.append(rs_start(f"s{k + 1}n{p}_", [corrected(field, 2, u)]))
            far_rs.append(rs_start(f"s{k + 1}f{p}_", [corrected(field, l, u) for l in range(3, nb)]))
        m01 = whole(m01s)
        if k + 1 < ROUNDS:
            q = partial(m01)
        else:
            out_ref[...] += b["x"][...] - expand(bhi, blo, cols(0, 2), m01)
        totals, ys = far_reduce(k + 1, far_rs)
        near_ag = [ag_start(f"s{k + 1}n{p}_ag", [rs_finish(f"s{k + 1}n{p}_", near_rs[p])[0]]) for p in parts]
        subs, far_ags = far_gather(k + 1, totals, ys)

    drain(17 * NH)
    moves = []
    for p in parts:
        g2 = ag_finish(f"s{ROUNDS}n{p}_ag", near_ag[p])[0]
        g3, g4 = ag_finish(f"s{ROUNDS}f{p}_ag", far_ags[p])
        moves.append(
            jnp.concatenate([moved_of(l, g) for l, g in ((2, g2), (3, g3), (4, g4))], axis=1)
        )
    out_ref[...] -= expand(bhi, blo, cols(2, NL), whole(moves))

    drain(0)


def body(rhs, leaf_block, leaf_inverse, level_basis, level_core, skeleton_basis, coupling):
    hbm = pl.BlockSpec(memory_space=pl.ANY)
    out = pl.pallas_call(
        kernel,
        out_shape=jax.ShapeDtypeStruct((M, R), F32),
        in_specs=[hbm] * 7,
        out_specs=pl.BlockSpec(memory_space=pltpu.VMEM),
        scratch_shapes=[
            *SCRATCH.values(),
            pltpu.SemaphoreType.DMA((NSEM,)),
            pltpu.SemaphoreType.DMA((NSEM,)),
        ],
        compiler_params=pltpu.CompilerParams(
            collective_id=0, has_side_effects=True, vmem_limit_bytes=56 * 2**20
        ),
        cost_estimate=pl.CostEstimate(flops=8 * 10**9, bytes_accessed=10 * 10**6, transcendentals=0),
        name="ridge_rounds",
    )(
        rhs[0, 0],
        leaf_block[0, 0],
        leaf_inverse[0, 0],
        level_basis[0, 0],
        level_core[0, 0],
        skeleton_basis[0, 0],
        coupling[0],
    )
    return out[None, None]


def solution(mesh):
    return jax.shard_map(
        body,
        mesh=mesh,
        in_specs=(
            P("sub", "leaf", None, None),
            P("sub", "leaf", None, None),
            P("sub", "leaf", None, None),
            P("sub", "leaf", None, None, None),
            P("sub", "leaf", None, None, None),
            P("sub", "leaf", None, None),
            P("sub", None, None, None),
        ),
        out_specs=P("sub", "leaf", None, None),
        check_vma=False,
    )
```
